32 devices in a mesh: groups: 2 (over y), seq: 4 (over z), dp: 4 (over x, core).
Axes of the slice: x: 2, y: 2, z: 4, core: 2. Of those that a mesh axis runs over, the one named last changes fastest.
Arguments:
- acceptance_gate: bfloat16 [8, 512, 1280], P(('groups', 'dp'), 'seq'), parts along dimension 0, may hold values from -6 to 6
- logarithmic_fade_factor: bfloat16 [8, 512, 1280], P(('groups', 'dp'), 'seq'), parts along dimension 0, may hold values from -12 to 0
- probe_matrix: bfloat16 [8, 512, 1280], P(('groups', 'dp'), 'seq'), parts along dimension 0, may hold values from -0.75 to 0.75
- payload_matrix: bfloat16 [8, 512, 1280], P(('groups', 'dp'), 'seq'), parts along dimension 0, may hold values from -6 to 6
- erasure_vector: bfloat16 [8, 512, 1280], P(('groups', 'dp'), 'seq'), parts along dimension 0, may hold values from -6 to 6
- inplace_update_step: bfloat16 [8, 512, 1280], P(('groups', 'dp'), 'seq'), parts along dimension 0, may hold values from 0.0079956055 to 0.019897461
- extra_probe_factor: float32 [1280], replicated, may hold values from -3 to 3
- group_scaling_factor: float32 [1280], replicated, may hold values from 0.5 to 1.5
Outputs:
- blended_signal: bfloat16 [8, 512, 1280], P(('groups', 'dp'), 'seq'), parts along dimension 0
- final_state: float32 [8, 1280, 64], P(('groups', 'dp'), 'seq'), parts along dimension 0
The draws below stay inside these ranges and needn't reach their ends.
There are 2 independent parts, one for each index of `groups`. The reference program is written for one: setup_inputs(seed, part) draws one part's arguments, and reference() takes and returns one part's arrays. A program takes and returns all parts, laid end to end along the dimension named above; an argument that names none is the same for every part. Nothing has to cross between parts.
All inputs are finite; a program needn't handle non-finite values.
Results may differ from the reference program's by a relative error of at most 0.001.
Values sent between devices are 32-bit elements; how exact they have to be, the bound alone decides.
A program may use at most 64 MiB of HBM per device.

```python
import jax
import jax.numpy as jnp
from jax import lax

GROUP_DIMENSION = 64
HEADS = 20
BLOCK = 64
TOKEN_COUNT = 512
BATCH_COUNT = 4
MODEL_DIMENSION = 1280


def draw_logarithmic_fade_factor(key, part):
    key_rows = jax.random.split(key, 6)
    fast_share = 0.5
    fast_head = jax.random.uniform(key_rows[0], (BATCH_COUNT, 1, HEADS, 1)) < fast_share
    span = jax.random.uniform(key_rows[1], (BATCH_COUNT, 1, HEADS, 1), minval=30.0, maxval=50.0)
    slow_rate = 2.302585 / TOKEN_COUNT * jax.random.uniform(key_rows[2], (BATCH_COUNT, 1, HEADS, 1), minval=0.1, maxval=0.4)
    base_rate = jnp.where(fast_head, 1.0 / span, slow_rate)
    rough = jnp.exp(jax.random.uniform(key_rows[3], (BATCH_COUNT, TOKEN_COUNT, HEADS, GROUP_DIMENSION), minval=-0.7, maxval=0.7))
    rate = base_rate * rough
    split_point = jax.random.randint(key_rows[4], (BATCH_COUNT, 1, 2), 0, TOKEN_COUNT)
    token_positions = jnp.arange(TOKEN_COUNT, dtype=jnp.int32).reshape(1, TOKEN_COUNT, 1)
    splitting_now = jnp.any(token_positions == split_point, axis=-1)[:, :, None, None]
    retained = jax.random.uniform(key_rows[5], (BATCH_COUNT, TOKEN_COUNT, HEADS, GROUP_DIMENSION), minval=0.5, maxval=0.8)
    rate = jnp.where(jnp.logical_and(splitting_now, jnp.logical_not(fast_head)), -jnp.log(retained), rate)
    return jnp.log(rate).reshape(BATCH_COUNT, TOKEN_COUNT, HEADS * GROUP_DIMENSION).astype(jnp.bfloat16)


def draw_erasure_vector(key, part):
    key_rows = jax.random.split(key, 2)
    block_total = TOKEN_COUNT // BLOCK
    common = jnp.clip(jax.random.normal(key_rows[0], (BATCH_COUNT, block_total, 1, HEADS, GROUP_DIMENSION)), -3.0, 3.0)
    jitter = 0.5 * jnp.clip(jax.random.normal(key_rows[1], (BATCH_COUNT, block_total, BLOCK, HEADS, GROUP_DIMENSION)), -3.0, 3.0)
    values = jnp.clip(common + jitter, -6.0, 6.0)
    return values.reshape(BATCH_COUNT, TOKEN_COUNT, HEADS * GROUP_DIMENSION).astype(jnp.bfloat16)


def level_of(stream_key, dims, pieces, low, high):
    gain = 1.0
    for axis_at, shards_of in pieces:
        heights = jax.random.uniform(jax.random.fold_in(jax.random.fold_in(stream_key, 6), axis_at), (shards_of,), jnp.float32, low / len(pieces), high / len(pieces))
        gain = gain * jnp.repeat(jnp.exp(heights), dims[axis_at] // shards_of).reshape((-1,) + (1,) * (len(dims) - 1 - axis_at))
    return gain


def centred(rng, shape, scale, most, cuts=(), kind=jnp.bfloat16):
    gain = level_of(rng, shape, cuts, -0.22, 0.18) if cuts else 1.0
    values = jax.random.normal(rng, shape, jnp.float32) * scale * gain
    return jnp.minimum(jnp.maximum(values, -most), most).astype(kind)


def setup_inputs(seed: int = 0, part: int = 0) -> dict:
    splits = jax.random.split(jax.random.key(seed), 9)
    part_keys = jax.random.split(jax.random.fold_in(splits[8], part), 9)
    acceptance_gate = centred(part_keys[0], (BATCH_COUNT, TOKEN_COUNT, MODEL_DIMENSION), 1.0, 6.0, ((0, 4), (1, 4)))
    logarithmic_fade_factor = draw_logarithmic_fade_factor(jax.random.fold_in(jax.random.fold_in(splits[8], part), 71), part)
    probe_matrix = centred(part_keys[2], (BATCH_COUNT, TOKEN_COUNT, MODEL_DIMENSION), 0.125, 0.75, ((0, 4), (1, 4)))
    payload_matrix = centred(part_keys[3], (BATCH_COUNT, TOKEN_COUNT, MODEL_DIMENSION), 1.0, 6.0, ((0, 4), (1, 4)))
    erasure_vector = draw_erasure_vector(jax.random.fold_in(jax.random.fold_in(splits[8], part), 71), part)
    inplace_update_step = jnp.clip(0.0079956055 + 0.0119018555 * jax.random.uniform(part_keys[5], (BATCH_COUNT, TOKEN_COUNT, MODEL_DIMENSION), jnp.float32) ** level_of(part_keys[5], (BATCH_COUNT, TOKEN_COUNT, MODEL_DIMENSION), ((0, 4), (1, 4)), -0.2, 0.2), 0.0079956055, 0.019897461).astype(jnp.bfloat16)
    extra_probe_factor = centred(splits[6], (MODEL_DIMENSION,), 0.5, 3.0, (), jnp.float32)
    group_scaling_factor = jnp.clip(1.0 + 0.1 * jax.random.normal(splits[7], (MODEL_DIMENSION,), jnp.float32), 0.5, 1.5)
    return dict(acceptance_gate=acceptance_gate, logarithmic_fade_factor=logarithmic_fade_factor, probe_matrix=probe_matrix, payload_matrix=payload_matrix, erasure_vector=erasure_vector, inplace_update_step=inplace_update_step, extra_probe_factor=extra_probe_factor, group_scaling_factor=group_scaling_factor)


HIGHEST_PRECISION = lax.Precision.HIGHEST
KEY_EPS = 1e-05
NORM_EPS = 0.00064

def reference(acceptance_gate, logarithmic_fade_factor, probe_matrix, payload_matrix, erasure_vector, inplace_update_step, extra_probe_factor, group_scaling_factor):
    series_entries, series_extent, feature_total = acceptance_gate.shape
    group_total = feature_total // GROUP_DIMENSION

    def grouped_entries(array):
        return array.astype(jnp.float32).reshape(series_entries, series_extent, group_total, GROUP_DIMENSION)
    removal = grouped_entries(erasure_vector)
    kappa = removal * lax.rsqrt(lax.optimization_barrier(jnp.mean(removal * removal, -1, keepdims=True)) + KEY_EPS) * GROUP_DIMENSION ** (-0.5)
    kappa_flat = kappa.reshape(series_entries, series_extent, feature_total)

    def time_major(array):
        return jnp.swapaxes(array, 0, 1)

    def split_heads(array):
        return array.astype(jnp.float32).reshape(series_entries, group_total, GROUP_DIMENSION)

    def advance(state_now, inputs):
        reader_t, decay_t, key_t, value_t, kappa_t, rate_t = inputs
        receptance_per_head = split_heads(reader_t)
        decay_h = jnp.exp(-jnp.exp(split_heads(decay_t)))
        key_per_head = split_heads(key_t)
        value_per_head = split_heads(value_t)
        kappa_h = split_heads(kappa_t)
        rate_h = split_heads(rate_t)
        pulled = jnp.einsum('bhvk,bhk->bhv', state_now, -kappa_h, precision=HIGHEST_PRECISION)
        state_now = state_now * decay_h[:, :, None, :] + pulled[..., None] * (kappa_h * rate_h)[:, :, None, :] + value_per_head[..., None] * key_per_head[:, :, None, :]
        result = jnp.einsum('bhvk,bhk->bhv', state_now, receptance_per_head, precision=HIGHEST_PRECISION)
        return (state_now, result)
    initial = jnp.zeros((series_entries, group_total, GROUP_DIMENSION, GROUP_DIMENSION), jnp.float32)
    closing, outputs = lax.scan(advance, initial, (time_major(acceptance_gate), time_major(logarithmic_fade_factor), time_major(probe_matrix), time_major(payload_matrix), time_major(kappa_flat), time_major(inplace_update_step)))
    outputs = jnp.swapaxes(outputs, 0, 1)
    average = lax.optimization_barrier(jnp.mean(outputs, -1, keepdims=True))
    centered = outputs - average
    spread = lax.optimization_barrier(jnp.mean(centered * centered, -1, keepdims=True))
    standardized_result = centered * lax.rsqrt(spread + NORM_EPS) * group_scaling_factor.reshape(group_total, GROUP_DIMENSION)
    extra_result = lax.optimization_barrier(jnp.sum(grouped_entries(acceptance_gate) * grouped_entries(probe_matrix) * extra_probe_factor.reshape(group_total, GROUP_DIMENSION), -1, keepdims=True)) * grouped_entries(payload_matrix)
    blended_signal = (standardized_result + extra_result).reshape(series_entries, series_extent, feature_total).astype(jnp.bfloat16)
    final_state = closing.reshape(series_entries, feature_total, GROUP_DIMENSION)
    return (blended_signal, final_state)
```

```python
import functools

import jax
import jax.numpy as jnp
from jax import lax
from jax.experimental import pallas as pl
from jax.experimental.pallas import tpu as pltpu
from jax.sharding import PartitionSpec as P

C = 64
LANES = 128
KEY_EPS = 1e-05
NORM_EPS = 0.00064
FINE_LEVELS = 4
GROUP = 2
F32 = jnp.float32
BF16 = jnp.bfloat16
MESH = pl.DeviceIdType.MESH


def split(x):
    hi = x.astype(BF16)
    return hi, (x - hi.astype(F32)).astype(BF16)


def dot(a, b):
    return lax.dot_general(a, b, (((1,), (0,)), ((), ())), preferred_element_type=F32)


def dot_t(a, b):
    return lax.dot_general(a, b, (((1,), (1,)), ((), ())), preferred_element_type=F32)


def cat(parts, axis):
    return jnp.concatenate(parts, axis)


def lane_ids(rows):
    return lax.broadcasted_iota(jnp.int32, (rows, LANES), 1)


def head_sum(x, ones2):
    hi, lo = split(x)
    return dot(cat([hi, lo], 1), ones2)


def head_ones():
    rows = lax.broadcasted_iota(jnp.int32, (2 * LANES, LANES), 0)
    cols = lax.broadcasted_iota(jnp.int32, (2 * LANES, LANES), 1)
    same = lax.rem(rows, LANES) // C == cols // C
    return jnp.where(same, 1.0, 0.0).astype(BF16)


def diagonal_state(z):
    first = lane_ids(C) < C
    return cat([jnp.where(first, z, 0.0), jnp.where(first, 0.0, z)], 0)


def product3(a, b):
    ahi, alo = split(a)
    bhi, blo = split(b)
    return dot(cat([ahi, alo], 1), cat([bhi, bhi], 0)) + dot(ahi, blo)


def kernel(
    members,
    r_ref, lf_ref, k_ref, v_ref, e_ref, a_ref, u_ref, g_ref,
    out_ref, final_ref,
    w_buf, add_buf, z_in, z_out, s_buf,
    send_sem, recv_sem, fsend_sem, frecv_sem, local_sem,
):
    T, channels = r_ref.shape
    pairs = channels // LANES
    groups = pairs // GROUP
    share = final_ref.shape[0]
    last = members - 1
    me = lax.axis_index("seq")
    barrier = pltpu.get_barrier_semaphore()
    for hop in range(1, members):
        pl.semaphore_signal(
            barrier, inc=1, device_id={"seq": lax.rem(me + hop, members)}, device_id_type=MESH
        )
    pl.semaphore_wait(barrier, members - 1)

    @pl.when(me == 0)
    def _():
        z_in[...] = jnp.zeros_like(z_in)

    def lanes_of(pair):
        return pl.ds(pl.multiple_of(pair * LANES, LANES), LANES)

    def compute(group):
        rows = lax.broadcasted_iota(jnp.int32, (T, T), 0)
        cols = lax.broadcasted_iota(jnp.int32, (T, T), 1)
        inclusive = rows >= cols
        strict = rows > cols
        lower = jnp.where(inclusive, 1.0, 0.0).astype(BF16)
        first = lane_ids(T) < C
        ones2 = head_ones()
        state_lanes = lane_ids(T + C) < C
        diag = lax.rem(lane_ids(C), C) == lax.broadcasted_iota(jnp.int32, (C, LANES), 0)
        heads = []
        ends = []
        for j in range(GROUP):
            at = lanes_of(group * GROUP + j)
            w = -jnp.exp(lf_ref[:, at].astype(F32))
            whi, wlo = split(w)
            both = dot(lower, cat([whi, wlo], 1))
            cum = both[:, :LANES] + both[:, LANES:]
            mid = cum[T // 2 - 1 : T // 2, :]
            end = cum[T - 1 : T, :]
            c = cum - mid
            e_c = jnp.exp(c)
            e_b = jnp.exp(c - w)
            e_inv = jnp.exp(-c)
            g_mid = jnp.exp(mid)
            g_end = jnp.exp(end - mid)
            gamma = jnp.exp(end)
            e = e_ref[:, at].astype(F32)
            kappa = e * lax.rsqrt(head_sum(e * e, ones2) * (1.0 / C) + KEY_EPS) * C**-0.5
            toward = -kappa * e_b
            reader = r_ref[:, at].astype(F32) * e_c
            away = kappa * a_ref[:, at].astype(F32) * e_inv
            keys = k_ref[:, at].astype(F32) * e_inv
            toward_true = toward * g_mid
            reader_true = reader * g_mid
            away_t = jnp.transpose(away * g_end)
            keys_t = jnp.transpose(keys * g_end)
            vroll = pltpu.roll(v_ref[:, at].astype(F32), C, 1)
            vroll_b = vroll.astype(BF16)
            vroll2 = cat([vroll_b, vroll_b], 0)
            qhi, qlo = split(cat([toward, reader], 0))
            q2 = cat([qhi, qlo], 1)
            ends.append((reader_true, jnp.where(diag, gamma, 0.0)))
            for h in range(2):
                own = first if h == 0 else jnp.logical_not(first)
                sides = cat([jnp.where(own, away, 0.0), jnp.where(own, keys, 0.0)], 0)
                khi, klo = split(sides)
                scores = dot_t(q2, cat([khi, khi], 1)) + dot_t(qhi, klo)
                mix_away = jnp.where(strict, scores[:T, :T], 0.0)
                mix_keys = jnp.where(strict, scores[:T, T:], 0.0)
                read = cat(
                    [
                        jnp.where(inclusive, scores[T:, :T], 0.0),
                        jnp.where(inclusive, scores[T:, T:], 0.0),
                    ],
                    1,
                )
                closing = cat([away_t[h * C : h * C + C], keys_t[h * C : h * C + C]], 1)
                mhi, mlo = split(mix_keys)
                mixed = dot(cat([mhi, mlo], 1), vroll2)
                heads.append(
                    dict(
                        y=mix_away,
                        x=jnp.where(own, toward_true, mixed),
                        left=cat([read, closing], 0),
                        v=jnp.where(own, 0.0, vroll).astype(BF16),
                    )
                )
        levels = (T - 1).bit_length()
        for level in range(levels):
            fine = level < FINE_LEVELS
            for head in heads:
                y, x = head["y"], head["x"]
                right = x if level == levels - 1 else cat([y, x], 1)
                if fine:
                    yhi, ylo = split(y)
                    rhi, rlo = split(right)
                    prod = dot(cat([yhi, ylo], 1), cat([rhi, rhi], 0)) + dot(yhi, rlo)
                else:
                    prod = dot(y.astype(BF16), right.astype(BF16))
                head["y"] = prod[:, :T]
                head["x"] = x + prod[:, -LANES:]
        for j in range(GROUP):
            results = []
            for head in heads[2 * j : 2 * j + 2]:
                lhi, llo = split(head["left"])
                xhi, xlo = split(head["x"])
                rhi = cat([xhi, head["v"]], 0)
                results.append(dot(lhi, rhi) + dot(llo, rhi) + dot(lhi[:, :T], xlo))
            pair = group * GROUP + j
            w_buf[pair] = jnp.where(state_lanes, results[0], results[1]) + cat(list(ends[j]), 0)
            add_buf[pair] = pltpu.roll(jnp.where(state_lanes, results[1], results[0]), C, 1)

    def state_copy(pair):
        return pltpu.make_async_remote_copy(
            src_ref=z_out.at[pair],
            dst_ref=z_in.at[pair],
            send_sem=send_sem.at[pair],
            recv_sem=recv_sem.at[pair],
            device_id={"seq": lax.rem(me + 1, members)},
            device_id_type=MESH,
        )

    def relay(group):
        for j in range(GROUP):
            pair = group * GROUP + j

            @pl.when(me > 0)
            def _():
                state_copy(pair).wait_recv()

            z = diagonal_state(z_in[pair])
            leaving = product3(w_buf[pair, T:, :], z) + add_buf[pair, T:, :]
            z_out[pair] = leaving

            @pl.when(me < last)
            def _():
                state_copy(pair).start()

            @pl.when(me == last)
            def _():
                s_buf[pl.ds(pl.multiple_of(pair * LANES, LANES), LANES), :] = jnp.transpose(leaving)

    def finish(group):
        ones2 = head_ones()
        for j in range(GROUP):
            pair = group * GROUP + j
            at = lanes_of(pair)
            z = diagonal_state(z_in[pair])
            result = product3(w_buf[pair, :T, :], z) + add_buf[pair, :T, :]
            average = head_sum(result, ones2) * (1.0 / C)
            centered = result - average
            spread = head_sum(centered * centered, ones2) * (1.0 / C)
            normed = centered * lax.rsqrt(spread + NORM_EPS) * g_ref[:, at]
            bonus = r_ref[:, at].astype(F32) * k_ref[:, at].astype(F32) * u_ref[:, at]
            extra = head_sum(bonus, ones2) * v_ref[:, at].astype(F32)
            out_ref[:, at] = (normed + extra).astype(out_ref.dtype)

    def step(s, _):
        @pl.when(s < groups)
        def _():
            compute(s)

        @pl.when(jnp.logical_and(s >= me, s - me < groups))
        def _():
            relay(s - me)

        return 0

    lax.fori_loop(0, groups + members - 1, step, 0)

    def final_copy(target):
        return pltpu.make_async_remote_copy(
            src_ref=s_buf.at[pl.ds(pl.multiple_of(target * share, 8), share), :],
            dst_ref=final_ref,
            send_sem=fsend_sem.at[target],
            recv_sem=frecv_sem,
            device_id={"seq": target},
            device_id_type=MESH,
        )

    @pl.when(me == last)
    def _():
        for target in range(last):
            final_copy(target).start()
        own = pltpu.make_async_copy(
            s_buf.at[pl.ds(last * share, share), :], final_ref, local_sem
        )
        own.start()
        own.wait()

    def finish_step(s, _):
        finish(s)
        return 0

    lax.fori_loop(0, groups, finish_step, 0)

    @pl.when(me == last)
    def _():
        for target in range(last):
            final_copy(target).wait_send()

    @pl.when(me < last)
    def _():
        final_copy(0).wait_recv()

        def sent(pair, _):
            state_copy(pair).wait_send()
            return 0

        lax.fori_loop(0, pairs, sent, 0)


def on_device(r, lf, k, v, e, a, u, g, *, members):
    sequences, T, channels = r.shape
    pairs = channels // LANES
    share = channels // members
    call = pl.pallas_call(
        functools.partial(kernel, members),
        out_shape=(
            jax.ShapeDtypeStruct((T, channels), BF16),
            jax.ShapeDtypeStruct((share, C), F32),
        ),
        in_specs=[pl.BlockSpec(memory_space=pltpu.VMEM)] * 8,
        out_specs=[pl.BlockSpec(memory_space=pltpu.VMEM)] * 2,
        scratch_shapes=[
            pltpu.VMEM((pairs, T + C, LANES), F32),
            pltpu.VMEM((pairs, T + C, LANES), F32),
            pltpu.VMEM((pairs, C, LANES), F32),
            pltpu.VMEM((pairs, C, LANES), F32),
            pltpu.VMEM((channels, C), F32),
            pltpu.SemaphoreType.DMA((pairs,)),
            pltpu.SemaphoreType.DMA((pairs,)),
            pltpu.SemaphoreType.DMA((members - 1,)),
            pltpu.SemaphoreType.DMA,
            pltpu.SemaphoreType.DMA,
        ],
        compiler_params=pltpu.CompilerParams(
            collective_id=0, has_side_effects=True, vmem_limit_bytes=48 * 1024 * 1024
        ),
    )
    out, final = call(
        *(x.reshape(T, channels) for x in (r, lf, k, v, e, a)),
        u.reshape(1, channels),
        g.reshape(1, channels),
    )
    return out.reshape(sequences, T, channels), final.reshape(sequences, share, C)


def solution(mesh):
    split_spec = P(("groups", "dp"), "seq", None)
    return jax.shard_map(
        functools.partial(on_device, members=mesh.shape["seq"]),
        mesh=mesh,
        in_specs=(split_spec,) * 6 + (P(), P()),
        out_specs=(split_spec, split_spec),
        check_vma=False,
    )
```

```python
import functools

import jax
import jax.numpy as jnp
from jax import lax
from jax.experimental import pallas as pl
from jax.experimental.pallas import tpu as pltpu
from jax.sharding import PartitionSpec as P

C = 64
LANES = 128
KEY_EPS = 1e-05
NORM_EPS = 0.00064
FINE_LEVELS = 3
GROUP = 2
F32 = jnp.float32
BF16 = jnp.bfloat16
MESH = pl.DeviceIdType.MESH


def split(x):
    hi = x.astype(BF16)
    return hi, (x - hi.astype(F32)).astype(BF16)


def dot(a, b):
    return lax.dot_general(a, b, (((1,), (0,)), ((), ())), preferred_element_type=F32)


def dot_t(a, b):
    return lax.dot_general(a, b, (((1,), (1,)), ((), ())), preferred_element_type=F32)


def cat(parts, axis):
    return jnp.concatenate(parts, axis)


def lane_ids(rows):
    return lax.broadcasted_iota(jnp.int32, (rows, LANES), 1)


def head_sum(x, ones2):
    hi, lo = split(x)
    return dot(cat([hi, lo], 1), ones2)


def head_ones():
    rows = lax.broadcasted_iota(jnp.int32, (2 * LANES, LANES), 0)
    cols = lax.broadcasted_iota(jnp.int32, (2 * LANES, LANES), 1)
    same = lax.rem(rows, LANES) // C == cols // C
    return jnp.where(same, 1.0, 0.0).astype(BF16)


def diagonal_state(z):
    first = lane_ids(C) < C
    return cat([jnp.where(first, z, 0.0), jnp.where(first, 0.0, z)], 0)


def product3(a, b):
    ahi, alo = split(a)
    bhi, blo = split(b)
    return dot(cat([ahi, alo, ahi], 1), cat([bhi, bhi, blo], 0))


def kernel(
    members,
    r_in, lf_in, k_in, v_in, e_in, a_in, u_in, g_in,
    out_ref, final_ref,
    r_ref, lf_ref, k_ref, v_ref, e_ref, a_ref, u_ref, g_ref,
    w_buf, add_buf, z_in, z_out, s_buf,
    send_sem, recv_sem, fsend_sem, frecv_sem, local_sem, in_sem, gain_sem,
):
    T, channels = r_ref.shape
    pairs = channels // LANES
    groups = pairs // GROUP
    share = final_ref.shape[0]
    last = members - 1
    me = lax.axis_index("seq")
    barrier = pltpu.get_barrier_semaphore()
    for hop in range(1, members):
        pl.semaphore_signal(
            barrier, inc=1, device_id={"seq": lax.rem(me + hop, members)}, device_id_type=MESH
        )

    arrays = (
        (r_in, r_ref), (lf_in, lf_ref), (k_in, k_ref), (v_in, v_ref), (e_in, e_ref), (a_in, a_ref)
    )
    gains = ((u_in, u_ref), (g_in, g_ref))

    def input_copies(group):
        at = pl.ds(pl.multiple_of(group * (GROUP * LANES), LANES), GROUP * LANES)
        return [
            pltpu.make_async_copy(source.at[:, at], target.at[:, at], in_sem.at[i, group])
            for i, (source, target) in enumerate(arrays)
        ]

    for group in range(groups):
        for copy in input_copies(group):
            copy.start()
    gain_copies = [
        pltpu.make_async_copy(source, target, gain_sem.at[i])
        for i, (source, target) in enumerate(gains)
    ]
    for copy in gain_copies:
        copy.start()

    @pl.when(me == 0)
    def _():
        z_in[...] = jnp.zeros_like(z_in)

    def lanes_of(pair):
        return pl.ds(pl.multiple_of(pair * LANES, LANES), LANES)

    def compute(group):
        for copy in input_copies(group):
            copy.wait()
        rows = lax.broadcasted_iota(jnp.int32, (T, T), 0)
        cols = lax.broadcasted_iota(jnp.int32, (T, T), 1)
        inclusive = rows >= cols
        strict = rows > cols
        lower = jnp.where(inclusive, 1.0, 0.0).astype(BF16)
        first = lane_ids(T) < C
        ones2 = head_ones()
        state_lanes = lane_ids(T + C) < C
        diag = lax.rem(lane_ids(C), C) == lax.broadcasted_iota(jnp.int32, (C, LANES), 0)
        heads = []
        ends = []
        for j in range(GROUP):
            at = lanes_of(group * GROUP + j)
            w = -jnp.exp(lf_ref[:, at].astype(F32))
            whi, wlo = split(w)
            both = dot(lower, cat([whi, wlo], 1))
            cum = both[:, :LANES] + both[:, LANES:]
            mid = cum[T // 2 - 1 : T // 2, :]
            end = cum[T - 1 : T, :]
            c = cum - mid
            e_c = jnp.exp(c)
            e_b = jnp.exp(c - w)
            e_inv = jnp.exp(-c)
            g_mid = jnp.exp(mid)
            g_end = jnp.exp(end - mid)
            gamma = jnp.exp(end)
            e = e_ref[:, at].astype(F32)
            kappa = e * lax.rsqrt(head_sum(e * e, ones2) * (1.0 / C) + KEY_EPS) * C**-0.5
            toward = -kappa * e_b
            reader = r_ref[:, at].astype(F32) * e_c
            away = kappa * a_ref[:, at].astype(F32) * e_inv
            keys = k_ref[:, at].astype(F32) * e_inv
            toward_true = toward * g_mid
            reader_true = reader * g_mid
            away_t = jnp.transpose(away * g_end)
            keys_t = jnp.transpose(keys * g_end)
            vroll = pltpu.roll(v_ref[:, at].astype(F32), C, 1)
            vroll_b = vroll.astype(BF16)
            vroll2 = cat([vroll_b, vroll_b], 0)
            qhi, qlo = split(cat([toward, reader], 0))
            q3 = cat([qhi, qlo, qhi], 1)
            ends.append((reader_true, jnp.where(diag, gamma, 0.0)))
            for h in range(2):
                own = first if h == 0 else jnp.logical_not(first)
                sides = cat([jnp.where(own, away, 0.0), jnp.where(own, keys, 0.0)], 0)
                khi, klo = split(sides)
                scores = dot_t(q3, cat([khi, khi, klo], 1))
                mix_away = jnp.where(strict, scores[:T, :T], 0.0)
                mix_keys = jnp.where(strict, scores[:T, T:], 0.0)
                read = cat(
                    [
                        jnp.where(inclusive, scores[T:, :T], 0.0),
                        jnp.where(inclusive, scores[T:, T:], 0.0),
                    ],
                    1,
                )
                closing = cat([away_t[h * C : h * C + C], keys_t[h * C : h * C + C]], 1)
                mhi, mlo = split(mix_keys)
                mixed = dot(cat([mhi, mlo], 1), vroll2)
                heads.append(
                    dict(
                        y=mix_away,
                        x=jnp.where(own, toward_true, mixed),
                        left=cat([read, closing], 0),
                        v=jnp.where(own, 0.0, vroll).astype(BF16),
                    )
                )
        levels = (T - 1).bit_length()
        for level in range(levels):
            fine = level < FINE_LEVELS
            for head in heads:
                y, x = head["y"], head["x"]
                right = x if level == levels - 1 else cat([y, x], 1)
                if fine:
                    yhi, ylo = split(y)
                    rhi, rlo = split(right)
                    prod = dot(cat([yhi, ylo, yhi], 1), cat([rhi, rhi, rlo], 0))
                else:
                    prod = dot(y.astype(BF16), right.astype(BF16))
                head["y"] = prod[:, :T]
                head["x"] = x + prod[:, -LANES:]
        for j in range(GROUP):
            results = []
            for head in heads[2 * j : 2 * j + 2]:
                lhi, llo = split(head["left"])
                xhi, xlo = split(head["x"])
                rhi = cat([xhi, head["v"]], 0)
                results.append(dot(cat([lhi, llo, lhi[:, :T]], 1), cat([rhi, rhi, xlo], 0)))
            pair = group * GROUP + j
            w_buf[pair] = jnp.where(state_lanes, results[0], results[1]) + cat(list(ends[j]), 0)
            add_buf[pair] = pltpu.roll(jnp.where(state_lanes, results[1], results[0]), C, 1)

    def state_copy(pair):
        return pltpu.make_async_remote_copy(
            src_ref=z_out.at[pair],
            dst_ref=z_in.at[pair],
            send_sem=send_sem.at[pair],
            recv_sem=recv_sem.at[pair],
            device_id={"seq": lax.rem(me + 1, members)},
            device_id_type=MESH,
        )

    def relay(group):
        for j in range(GROUP):
            pair = group * GROUP + j

            @pl.when(me > 0)
            def _():
                state_copy(pair).wait_recv()

            z = diagonal_state(z_in[pair])
            leaving = product3(w_buf[pair, T:, :], z) + add_buf[pair, T:, :]
            z_out[pair] = leaving

            @pl.when(me < last)
            def _():
                state_copy(pair).start()

            @pl.when(me == last)
            def _():
                s_buf[pl.ds(pl.multiple_of(pair * LANES, LANES), LANES), :] = jnp.transpose(leaving)

    def finish(group):
        ones2 = head_ones()
        for j in range(GROUP):
            pair = group * GROUP + j
            at = lanes_of(pair)
            z = diagonal_state(z_in[pair])
            result = product3(w_buf[pair, :T, :], z) + add_buf[pair, :T, :]
            average = head_sum(result, ones2) * (1.0 / C)
            centered = result - average
            spread = head_sum(centered * centered, ones2) * (1.0 / C)
            normed = centered * lax.rsqrt(spread + NORM_EPS) * g_ref[:, at]
            bonus = r_ref[:, at].astype(F32) * k_ref[:, at].astype(F32) * u_ref[:, at]
            extra = head_sum(bonus, ones2) * v_ref[:, at].astype(F32)
            out_ref[:, at] = (normed + extra).astype(out_ref.dtype)

    def final_copy(target):
        return pltpu.make_async_remote_copy(
            src_ref=s_buf.at[pl.ds(pl.multiple_of(target * share, 8), share), :],
            dst_ref=final_ref,
            send_sem=fsend_sem.at[target],
            recv_sem=frecv_sem,
            device_id={"seq": target},
            device_id_type=MESH,
        )

    def own_copy():
        return pltpu.make_async_copy(s_buf.at[pl.ds(last * share, share), :], final_ref, local_sem)

    group_rows = GROUP * LANES
    finish_from = jnp.maximum(me + 1, groups - (me // last) * groups)

    def step(s, _):
        @pl.when(s < groups)
        def _():
            compute(s)

        @pl.when(s == 0)
        def _():
            pl.semaphore_wait(barrier, members - 1)
            for copy in gain_copies:
                copy.wait()

        done = s - finish_from

        @pl.when(jnp.logical_and(done >= 0, done < groups))
        def _():
            finish(done)

        turn = s - me

        @pl.when(jnp.logical_and(turn >= 0, turn < groups))
        def _():
            relay(turn)

            @pl.when(me == last)
            def _():
                for target in range(last):
                    ready = -(-(target + 1) * share // group_rows) - 1

                    @pl.when(turn == ready)
                    def _():
                        final_copy(target).start()

                @pl.when(turn == groups - 1)
                def _():
                    own_copy().start()

        return 0

    lax.fori_loop(0, groups + max(groups, members), step, 0)

    @pl.when(me == last)
    def _():
        own_copy().wait()
        for target in range(last):
            final_copy(target).wait_send()

    @pl.when(me < last)
    def _():
        final_copy(0).wait_recv()

        def sent(pair, _):
            state_copy(pair).wait_send()
            return 0

        lax.fori_loop(0, pairs, sent, 0)


def on_device(r, lf, k, v, e, a, u, g, *, members):
    sequences, T, channels = r.shape
    pairs = channels // LANES
    share = channels // members
    call = pl.pallas_call(
        functools.partial(kernel, members),
        out_shape=(
            jax.ShapeDtypeStruct((T, channels), BF16),
            jax.ShapeDtypeStruct((share, C), F32),
        ),
        in_specs=[pl.BlockSpec(memory_space=pl.ANY)] * 8,
        out_specs=[pl.BlockSpec(memory_space=pltpu.VMEM)] * 2,
        scratch_shapes=[pltpu.VMEM((T, channels), BF16)] * 6
        + [pltpu.VMEM((1, channels), F32)] * 2
        + [
            pltpu.VMEM((pairs, T + C, LANES), F32),
            pltpu.VMEM((pairs, T + C, LANES), F32),
            pltpu.VMEM((pairs, C, LANES), F32),
            pltpu.VMEM((pairs, C, LANES), F32),
            pltpu.VMEM((channels, C), F32),
            pltpu.SemaphoreType.DMA((pairs,)),
            pltpu.SemaphoreType.DMA((pairs,)),
            pltpu.SemaphoreType.DMA((members - 1,)),
            pltpu.SemaphoreType.DMA,
            pltpu.SemaphoreType.DMA,
            pltpu.SemaphoreType.DMA((6, pairs // GROUP)),
            pltpu.SemaphoreType.DMA((2,)),
        ],
        compiler_params=pltpu.CompilerParams(
            collective_id=0, has_side_effects=True, vmem_limit_bytes=60 * 1024 * 1024
        ),
    )
    out, final = call(
        *(x.reshape(T, channels) for x in (r, lf, k, v, e, a)),
        u.reshape(1, channels),
        g.reshape(1, channels),
    )
    return out.reshape(sequences, T, channels), final.reshape(sequences, share, C)


def solution(mesh):
    split_spec = P(("groups", "dp"), "seq", None)
    return jax.shard_map(
        functools.partial(on_device, members=mesh.shape["seq"]),
        mesh=mesh,
        in_specs=(split_spec,) * 6 + (P(), P()),
        out_specs=(split_spec, split_spec),
        check_vma=False,
    )
```

```python
import functools

import jax
import jax.numpy as jnp
from jax import lax
from jax.experimental import pallas as pl
from jax.experimental.pallas import tpu as pltpu
from jax.sharding import PartitionSpec as P

C = 64
LANES = 128
KEY_EPS = 1e-05
NORM_EPS = 0.00064
FINE_LEVELS = 3
GROUP = 5
F32 = jnp.float32
BF16 = jnp.bfloat16
MESH = pl.DeviceIdType.MESH


def split(x):
    hi = x.astype(BF16)
    return hi, (x - hi.astype(F32)).astype(BF16)


def dot(a, b):
    return lax.dot_general(a, b, (((1,), (0,)), ((), ())), preferred_element_type=F32)


def dot_t(a, b):
    return lax.dot_general(a, b, (((1,), (1,)), ((), ())), preferred_element_type=F32)


def cat(parts, axis):
    return jnp.concatenate(parts, axis)


def lane_ids(rows):
    return lax.broadcasted_iota(jnp.int32, (rows, LANES), 1)


def head_sum(x, ones2):
    hi, lo = split(x)
    return dot(cat([hi, lo], 1), ones2)


def head_ones():
    rows = lax.broadcasted_iota(jnp.int32, (2 * LANES, LANES), 0)
    cols = lax.broadcasted_iota(jnp.int32, (2 * LANES, LANES), 1)
    same = lax.rem(rows, LANES) // C == cols // C
    return jnp.where(same, 1.0, 0.0).astype(BF16)


def diagonal_state(z):
    first = lane_ids(C) < C
    return cat([jnp.where(first, z, 0.0), jnp.where(first, 0.0, z)], 0)


def product3(a, b):
    ahi, alo = split(a)
    bhi, blo = split(b)
    return dot(cat([ahi, alo, ahi], 1), cat([bhi, bhi, blo], 0))


def kernel(
    members,
    r_in, lf_in, k_in, v_in, e_in, a_in, u_ref, g_ref,
    out_ref, final_ref,
    r_ref, lf_ref, k_ref, v_ref, e_ref, a_ref,
    w_buf, add_buf, z_in, z_out, s_buf,
    send_sem, recv_sem, fsend_sem, frecv_sem, local_sem, in_sem,
):
    T, channels = r_ref.shape
    pairs = channels // LANES
    groups = pairs // GROUP
    share = final_ref.shape[0]
    last = members - 1
    me = lax.axis_index("seq")
    barrier = pltpu.get_barrier_semaphore()
    for hop in range(1, members):
        pl.semaphore_signal(
            barrier, inc=1, device_id={"seq": lax.rem(me + hop, members)}, device_id_type=MESH
        )

    arrays = (
        (r_in, r_ref), (lf_in, lf_ref), (k_in, k_ref), (v_in, v_ref), (e_in, e_ref), (a_in, a_ref)
    )

    def input_copies(group):
        at = pl.ds(pl.multiple_of(group * (GROUP * LANES), LANES), GROUP * LANES)
        return [
            pltpu.make_async_copy(source.at[:, at], target.at[:, at], in_sem.at[i, group])
            for i, (source, target) in enumerate(arrays)
        ]

    for group in range(groups):
        for copy in input_copies(group):
            copy.start()

    @pl.when(me == 0)
    def _():
        z_in[...] = jnp.zeros_like(z_in)

    def lanes_of(pair):
        return pl.ds(pl.multiple_of(pair * LANES, LANES), LANES)

    def compute(group):
        for copy in input_copies(group):
            copy.wait()
        rows = lax.broadcasted_iota(jnp.int32, (T, T), 0)
        cols = lax.broadcasted_iota(jnp.int32, (T, T), 1)
        inclusive = rows >= cols
        strict = rows > cols
        lower = jnp.where(inclusive, 1.0, 0.0).astype(BF16)
        first = lane_ids(T) < C
        ones2 = head_ones()
        state_lanes = lane_ids(T + C) < C
        diag = lax.rem(lane_ids(C), C) == lax.broadcasted_iota(jnp.int32, (C, LANES), 0)
        heads = []
        ends = []
        for j in range(GROUP):
            at = lanes_of(group * GROUP + j)
            w = -jnp.exp(lf_ref[:, at].astype(F32))
            whi, wlo = split(w)
            both = dot(lower, cat([whi, wlo], 1))
            cum = both[:, :LANES] + both[:, LANES:]
            mid = cum[T // 2 - 1 : T // 2, :]
            end = cum[T - 1 : T, :]
            c = cum - mid
            e_c = jnp.exp(c)
            e_b = jnp.exp(c - w)
            e_inv = jnp.exp(-c)
            g_mid = jnp.exp(mid)
            g_end = jnp.exp(end - mid)
            gamma = jnp.exp(end)
            e = e_ref[:, at].astype(F32)
            kappa = e * lax.rsqrt(head_sum(e * e, ones2) * (1.0 / C) + KEY_EPS) * C**-0.5
            toward = -kappa * e_b
            reader = r_ref[:, at].astype(F32) * e_c
            away = kappa * a_ref[:, at].astype(F32) * e_inv
            keys = k_ref[:, at].astype(F32) * e_inv
            toward_true = toward * g_mid
            reader_true = reader * g_mid
            away_t = jnp.transpose(away * g_end)
            keys_t = jnp.transpose(keys * g_end)
            vroll = pltpu.roll(v_ref[:, at].astype(F32), C, 1)
            vroll_b = vroll.astype(BF16)
            vroll2 = cat([vroll_b, vroll_b], 0)
            qhi, qlo = split(cat([toward, reader], 0))
            q3 = cat([qhi, qlo, qhi], 1)
            ends.append((reader_true, jnp.where(diag, gamma, 0.0)))
            for h in range(2):
                own = first if h == 0 else jnp.logical_not(first)
                sides = cat([jnp.where(own, away, 0.0), jnp.where(own, keys, 0.0)], 0)
                khi, klo = split(sides)
                scores = dot_t(q3, cat([khi, khi, klo], 1))
                mix_away = jnp.where(strict, scores[:T, :T], 0.0)
                mix_keys = jnp.where(strict, scores[:T, T:], 0.0)
                read = cat(
                    [
                        jnp.where(inclusive, scores[T:, :T], 0.0),
                        jnp.where(inclusive, scores[T:, T:], 0.0),
                    ],
                    1,
                )
                closing = cat([away_t[h * C : h * C + C], keys_t[h * C : h * C + C]], 1)
                mhi, mlo = split(mix_keys)
                mixed = dot(cat([mhi, mlo], 1), vroll2)
                heads.append(
                    dict(
                        y=mix_away,
                        x=jnp.where(own, toward_true, mixed),
                        left=cat([read, closing], 0),
                        v=jnp.where(own, 0.0, vroll).astype(BF16),
                    )
                )
        levels = (T - 1).bit_length()
        for level in range(levels):
            fine = level < FINE_LEVELS
            skip = 2**level if 2**level >= 16 else 0
            later = 2 ** (level + 1) if 2 ** (level + 1) >= 16 else 0
            for head in heads:
                y, x = head["y"], head["x"]
                if fine:
                    yhi, ylo = split(y)
                    rhi, rlo = split(cat([y, x], 1))
                    prod = dot(cat([yhi, ylo, yhi], 1), cat([rhi, rhi, rlo], 0))
                else:
                    y, right = y.astype(BF16), x.astype(BF16)
                    if level < levels - 1:
                        full = cat([jnp.zeros((skip, T), BF16), y], 0) if skip else y
                        right = cat([full, right], 1)
                    prod = dot(y, right)
                if level < levels - 1:
                    head["y"] = prod[later - skip :, :T]
                gained = prod[:, -LANES:]
                head["x"] = cat([x[:skip], x[skip:] + gained], 0) if skip else x + gained
        for j in range(GROUP):
            results = []
            for head in heads[2 * j : 2 * j + 2]:
                lhi, llo = split(head["left"])
                xhi, xlo = split(head["x"])
                rhi = cat([xhi, head["v"]], 0)
                results.append(dot(cat([lhi, llo, lhi[:, :T]], 1), cat([rhi, rhi, xlo], 0)))
            pair = group * GROUP + j
            w_buf[pair] = jnp.where(state_lanes, results[0], results[1]) + cat(list(ends[j]), 0)
            add_buf[pair] = pltpu.roll(jnp.where(state_lanes, results[1], results[0]), C, 1)

    def state_copy(pair):
        return pltpu.make_async_remote_copy(
            src_ref=z_out.at[pair],
            dst_ref=z_in.at[pair],
            send_sem=send_sem.at[pair],
            recv_sem=recv_sem.at[pair],
            device_id={"seq": lax.rem(me + 1, members)},
            device_id_type=MESH,
        )

    def relay(group):
        for j in range(GROUP):
            pair = group * GROUP + j

            @pl.when(me == 0)
            def _():
                z_out[pair] = add_buf[pair, T:, :]

            @pl.when(me > 0)
            def _():
                state_copy(pair).wait_recv()
                z = diagonal_state(z_in[pair])
                z_out[pair] = product3(w_buf[pair, T:, :], z) + add_buf[pair, T:, :]

            @pl.when(me < last)
            def _():
                state_copy(pair).start()

            @pl.when(me == last)
            def _():
                s_buf[pl.ds(pl.multiple_of(pair * LANES, LANES), LANES), :] = jnp.transpose(
                    z_out[pair]
                )

    def finish(group):
        ones2 = head_ones()
        for j in range(GROUP):
            pair = group * GROUP + j
            at = lanes_of(pair)
            z = diagonal_state(z_in[pair])
            result = product3(w_buf[pair, :T, :], z) + add_buf[pair, :T, :]
            average = head_sum(result, ones2) * (1.0 / C)
            centered = result - average
            spread = head_sum(centered * centered, ones2) * (1.0 / C)
            normed = centered * lax.rsqrt(spread + NORM_EPS) * g_ref[:, at]
            bonus = r_ref[:, at].astype(F32) * k_ref[:, at].astype(F32) * u_ref[:, at]
            extra = head_sum(bonus, ones2) * v_ref[:, at].astype(F32)
            out_ref[:, at] = (normed + extra).astype(out_ref.dtype)

    def final_copy(target):
        return pltpu.make_async_remote_copy(
            src_ref=s_buf.at[pl.ds(pl.multiple_of(target * share, 8), share), :],
            dst_ref=final_ref,
            send_sem=fsend_sem.at[target],
            recv_sem=frecv_sem,
            device_id={"seq": target},
            device_id_type=MESH,
        )

    def own_copy():
        return pltpu.make_async_copy(s_buf.at[pl.ds(last * share, share), :], final_ref, local_sem)

    group_rows = GROUP * LANES
    finish_from = jnp.maximum(me + 1, groups - (me // last) * groups)

    def step(s, _):
        @pl.when(s < groups)
        def _():
            compute(s)

        @pl.when(s == 0)
        def _():
            pl.semaphore_wait(barrier, members - 1)

        done = s - finish_from

        @pl.when(jnp.logical_and(done >= 0, done < groups))
        def _():
            finish(done)

        turn = s - me

        @pl.when(jnp.logical_and(turn >= 0, turn < groups))
        def _():
            relay(turn)

            @pl.when(me == last)
            def _():
                for target in range(last):
                    ready = -(-(target + 1) * share // group_rows) - 1

                    @pl.when(turn == ready)
                    def _():
                        final_copy(target).start()

                @pl.when(turn == groups - 1)
                def _():
                    own_copy().start()

        return 0

    lax.fori_loop(0, groups + max(groups, members), step, 0)

    @pl.when(me == last)
    def _():
        own_copy().wait()
        for target in range(last):
            final_copy(target).wait_send()

    @pl.when(me < last)
    def _():
        final_copy(0).wait_recv()

        def sent(pair, _):
            state_copy(pair).wait_send()
            return 0

        lax.fori_loop(0, pairs, sent, 0)


def on_device(r, lf, k, v, e, a, u, g, *, members):
    sequences, T, channels = r.shape
    pairs = channels // LANES
    share = channels // members
    call = pl.pallas_call(
        functools.partial(kernel, members),
        out_shape=(
            jax.ShapeDtypeStruct((T, channels), BF16),
            jax.ShapeDtypeStruct((share, C), F32),
        ),
        in_specs=[pl.BlockSpec(memory_space=pltpu.HBM)] * 6
        + [pl.BlockSpec(memory_space=pltpu.VMEM)] * 2,
        out_specs=[pl.BlockSpec(memory_space=pltpu.VMEM)] * 2,
        scratch_shapes=[pltpu.VMEM((T, channels), BF16)] * 6
        + [
            pltpu.VMEM((pairs, T + C, LANES), F32),
            pltpu.VMEM((pairs, T + C, LANES), F32),
            pltpu.VMEM((pairs, C, LANES), F32),
            pltpu.VMEM((pairs, C, LANES), F32),
            pltpu.VMEM((channels, C), F32),
            pltpu.SemaphoreType.DMA((pairs,)),
            pltpu.SemaphoreType.DMA((pairs,)),
            pltpu.SemaphoreType.DMA((members - 1,)),
            pltpu.SemaphoreType.DMA,
            pltpu.SemaphoreType.DMA,
            pltpu.SemaphoreType.DMA((6, pairs // GROUP)),
        ],
        compiler_params=pltpu.CompilerParams(
            collective_id=0, has_side_effects=True, vmem_limit_bytes=40 * 1024 * 1024
        ),
    )
    out, final = call(
        *(x.reshape(T, channels) for x in (r, lf, k, v, e, a)),
        u.reshape(1, channels),
        g.reshape(1, channels),
    )
    return out.reshape(sequences, T, channels), final.reshape(sequences, share, C)


def solution(mesh):
    split_spec = P(("groups", "dp"), "seq", None)
    return jax.shard_map(
        functools.partial(on_device, members=mesh.shape["seq"]),
        mesh=mesh,
        in_specs=(split_spec,) * 6 + (P(), P()),
        out_specs=(split_spec, split_spec),
        check_vma=False,
    )
```

```python
import functools

import jax
import jax.numpy as jnp
from jax import lax
from jax.experimental import pallas as pl
from jax.experimental.pallas import tpu as pltpu
from jax.sharding import PartitionSpec as P

C = 64
LANES = 128
KEY_EPS = 1e-05
NORM_EPS = 0.00064
FINE_LEVELS = 3
GROUP = 2
PIECES = 4
VMEM_GRANT = 60 * 1024 * 1024
F32 = jnp.float32
BF16 = jnp.bfloat16
MESH = pl.DeviceIdType.MESH


def split(x):
    hi = x.astype(BF16)
    return hi, (x - hi.astype(F32)).astype(BF16)


def dot(a, b):
    return lax.dot_general(a, b, (((1,), (0,)), ((), ())), preferred_element_type=F32)


def dot_t(a, b):
    return lax.dot_general(a, b, (((1,), (1,)), ((), ())), preferred_element_type=F32)


def cat(parts, axis):
    return jnp.concatenate(parts, axis)


def lane_ids(rows):
    return lax.broadcasted_iota(jnp.int32, (rows, LANES), 1)


def head_sum(x, ones2):
    hi, lo = split(x)
    return dot(cat([hi, lo], 1), ones2)


def head_ones():
    rows = lax.broadcasted_iota(jnp.int32, (2 * LANES, LANES), 0)
    cols = lax.broadcasted_iota(jnp.int32, (2 * LANES, LANES), 1)
    same = lax.rem(rows, LANES) // C == cols // C
    return jnp.where(same, 1.0, 0.0).astype(BF16)


def diagonal_state(z):
    first = lane_ids(C) < C
    return cat([jnp.where(first, z, 0.0), jnp.where(first, 0.0, z)], 0)


def product3(a, b):
    ahi, alo = split(a)
    bhi, blo = split(b)
    return dot(cat([ahi, alo, ahi], 1), cat([bhi, bhi, blo], 0))


def kernel(
    members,
    r_in, lf_in, k_in, v_in, e_in, a_in, u_in, g_in,
    out_hbm, final_ref,
    r_ref, lf_ref, k_ref, v_ref, e_ref, a_ref, u_ref, g_ref, out_ref,
    w_buf, add_buf, z_in, z_out, s_buf,
    send_sem, recv_sem, fsend_sem, frecv_sem, local_sem, in_sem, gain_sem, out_sem,
):
    T, channels = r_ref.shape
    pairs = channels // LANES
    groups = pairs // GROUP
    share = final_ref.shape[0]
    last = members - 1
    me = lax.axis_index("seq")
    barrier = pltpu.get_barrier_semaphore()
    for hop in range(1, members):
        pl.semaphore_signal(
            barrier, inc=1, device_id={"seq": lax.rem(me + hop, members)}, device_id_type=MESH
        )

    arrays = (
        (r_in, r_ref), (lf_in, lf_ref), (k_in, k_ref), (v_in, v_ref), (e_in, e_ref), (a_in, a_ref)
    )

    def input_copies(group):
        at = pl.ds(pl.multiple_of(group * (GROUP * LANES), LANES), GROUP * LANES)
        return [
            pltpu.make_async_copy(source.at[:, at], target.at[:, at], in_sem.at[i, group])
            for i, (source, target) in enumerate(arrays)
        ]

    for group in range(groups):
        for copy in input_copies(group):
            copy.start()
    gain_copies = [
        pltpu.make_async_copy(source, target, gain_sem.at[i])
        for i, (source, target) in enumerate(((u_in, u_ref), (g_in, g_ref)))
    ]
    for copy in gain_copies:
        copy.start()

    @pl.when(me == 0)
    def _():
        z_in[...] = jnp.zeros_like(z_in)

    def lanes_of(pair):
        return pl.ds(pl.multiple_of(pair * LANES, LANES), LANES)

    def compute(group):
        for copy in input_copies(group):
            copy.wait()
        rows = lax.broadcasted_iota(jnp.int32, (T, T), 0)
        cols = lax.broadcasted_iota(jnp.int32, (T, T), 1)
        inclusive = rows >= cols
        strict = rows > cols
        lower = jnp.where(inclusive, 1.0, 0.0).astype(BF16)
        first = lane_ids(T) < C
        ones2 = head_ones()
        state_lanes = lane_ids(T + C) < C
        diag = lax.rem(lane_ids(C), C) == lax.broadcasted_iota(jnp.int32, (C, LANES), 0)
        heads = []
        ends = []
        for j in range(GROUP):
            at = lanes_of(group * GROUP + j)
            w = -jnp.exp(lf_ref[:, at].astype(F32))
            whi, wlo = split(w)
            both = dot(lower, cat([whi, wlo], 1))
            cum = both[:, :LANES] + both[:, LANES:]
            mid = cum[T // 2 - 1 : T // 2, :]
            end = cum[T - 1 : T, :]
            c = cum - mid
            e_c = jnp.exp(c)
            e_b = jnp.exp(c - w)
            e_inv = jnp.exp(-c)
            g_mid = jnp.exp(mid)
            g_end = jnp.exp(end - mid)
            gamma = jnp.exp(end)
            e = e_ref[:, at].astype(F32)
            kappa = e * lax.rsqrt(head_sum(e * e, ones2) * (1.0 / C) + KEY_EPS) * C**-0.5
            toward = -kappa * e_b
            reader = r_ref[:, at].astype(F32) * e_c
            away = kappa * a_ref[:, at].astype(F32) * e_inv
            keys = k_ref[:, at].astype(F32) * e_inv
            toward_true = toward * g_mid
            reader_true = reader * g_mid
            away_t = jnp.transpose(away * g_end)
            keys_t = jnp.transpose(keys * g_end)
            vroll = pltpu.roll(v_ref[:, at].astype(F32), C, 1)
            vroll_b = vroll.astype(BF16)
            vroll2 = cat([vroll_b, vroll_b], 0)
            first2 = lane_ids(2 * T) < C
            query = cat([toward, reader], 0)
            qhi = query.astype(BF16)
            qlo_r = pltpu.roll(query - qhi.astype(F32), C, 1).astype(BF16)
            sides = cat([away, keys], 0)
            khi = sides.astype(BF16)
            klo = (sides - khi.astype(F32)).astype(BF16)
            khi_r = pltpu.roll(khi.astype(F32), C, 1).astype(BF16)
            ends.append((reader_true, jnp.where(diag, gamma, 0.0)))
            for h in range(2):
                own = first if h == 0 else jnp.logical_not(first)
                own2 = first2 if h == 0 else jnp.logical_not(first2)
                scores = dot_t(
                    cat([jnp.where(own2, qhi, qlo_r), qhi], 1),
                    cat([jnp.where(own2, khi, khi_r), jnp.where(own2, klo, jnp.zeros_like(klo))], 1),
                )
                mix_away = jnp.where(strict, scores[:T, :T], 0.0)
                mix_keys = jnp.where(strict, scores[:T, T:], 0.0)
                read = cat(
                    [
                        jnp.where(inclusive, scores[T:, :T], 0.0),
                        jnp.where(inclusive, scores[T:, T:], 0.0),
                    ],
                    1,
                )
                closing = cat([away_t[h * C : h * C + C], keys_t[h * C : h * C + C]], 1)
                mhi, mlo = split(mix_keys)
                mixed = dot(cat([mhi, mlo], 1), vroll2)
                heads.append(
                    dict(
                        y=mix_away,
                        x=jnp.where(own, toward_true, mixed),
                        left=cat([read, closing], 0),
                        v=jnp.where(own, 0.0, vroll).astype(BF16),
                    )
                )
        levels = (T - 1).bit_length()
        for level in range(levels):
            fine = level < FINE_LEVELS
            skip = 2**level if 2**level >= 16 else 0
            later = 2 ** (level + 1) if 2 ** (level + 1) >= 16 else 0
            for head in heads:
                y, x = head["y"], head["x"]
                if fine:
                    yhi, ylo = split(y)
                    rhi, rlo = split(cat([y, x], 1))
                    prod = dot(cat([yhi, ylo, yhi], 1), cat([rhi, rhi, rlo], 0))
                else:
                    y, right = y.astype(BF16), x.astype(BF16)
                    if level < levels - 1:
                        full = cat([jnp.zeros((skip, T), BF16), y], 0) if skip else y
                        right = cat([full, right], 1)
                    prod = dot(y, right)
                if level < levels - 1:
                    head["y"] = prod[later - skip :, :T]
                gained = prod[:, -LANES:]
                head["x"] = cat([x[:skip], x[skip:] + gained], 0) if skip else x + gained
        for j in range(GROUP):
            results = []
            for head in heads[2 * j : 2 * j + 2]:
                lhi, llo = split(head["left"])
                xhi, xlo = split(head["x"])
                rhi = cat([xhi, head["v"]], 0)
                results.append(dot(cat([lhi, llo, lhi[:, :T]], 1), cat([rhi, rhi, xlo], 0)))
            pair = group * GROUP + j
            w_buf[pair] = jnp.where(state_lanes, results[0], results[1]) + cat(list(ends[j]), 0)
            add_buf[pair] = pltpu.roll(jnp.where(state_lanes, results[1], results[0]), C, 1)

    def state_copy(pair):
        return pltpu.make_async_remote_copy(
            src_ref=z_out.at[pair],
            dst_ref=z_in.at[pair],
            send_sem=send_sem.at[pair],
            recv_sem=recv_sem.at[pair],
            device_id={"seq": lax.rem(me + 1, members)},
            device_id_type=MESH,
        )

    def relay(group):
        for j in range(GROUP):
            pair = group * GROUP + j

            @pl.when(me == 0)
            def _():
                z_out[pair] = add_buf[pair, T:, :]

            @pl.when(me > 0)
            def _():
                state_copy(pair).wait_recv()
                z = diagonal_state(z_in[pair])
                z_out[pair] = product3(w_buf[pair, T:, :], z) + add_buf[pair, T:, :]

            @pl.when(me < last)
            def _():
                state_copy(pair).start()

            @pl.when(me == last)
            def _():
                s_buf[pl.ds(pl.multiple_of(pair * LANES, LANES), LANES), :] = jnp.transpose(
                    z_out[pair]
                )

    def out_copy(group):
        at = pl.ds(pl.multiple_of(group * (GROUP * LANES), LANES), GROUP * LANES)
        return pltpu.make_async_copy(out_ref.at[:, at], out_hbm.at[:, at], out_sem.at[group])

    def finish(group):
        ones2 = head_ones()
        for j in range(GROUP):
            pair = group * GROUP + j
            at = lanes_of(pair)
            z = diagonal_state(z_in[pair])
            result = product3(w_buf[pair, :T, :], z) + add_buf[pair, :T, :]
            average = head_sum(result, ones2) * (1.0 / C)
            centered = result - average
            spread = head_sum(centered * centered, ones2) * (1.0 / C)
            normed = centered * lax.rsqrt(spread + NORM_EPS) * g_ref[at][None, :]
            bonus = r_ref[:, at].astype(F32) * k_ref[:, at].astype(F32) * u_ref[at][None, :]
            extra = head_sum(bonus, ones2) * v_ref[:, at].astype(F32)
            out_ref[:, at] = (normed + extra).astype(out_ref.dtype)
        out_copy(group).start()

    def final_copy(target):
        return pltpu.make_async_remote_copy(
            src_ref=s_buf.at[pl.ds(pl.multiple_of(target * share, 8), share), :],
            dst_ref=final_ref,
            send_sem=fsend_sem.at[target],
            recv_sem=frecv_sem,
            device_id={"seq": target},
            device_id_type=MESH,
        )

    def own_copy():
        return pltpu.make_async_copy(s_buf.at[pl.ds(last * share, share), :], final_ref, local_sem)

    group_rows = GROUP * LANES
    finish_from = jnp.maximum(me + 1, groups - (me // last) * groups)

    def step(s, _):
        @pl.when(s < groups)
        def _():
            compute(s)

        @pl.when(s == 0)
        def _():
            pl.semaphore_wait(barrier, members - 1)
            for copy in gain_copies:
                copy.wait()

        done = s - finish_from

        @pl.when(jnp.logical_and(done >= 0, done < groups))
        def _():
            finish(done)

        turn = s - me

        @pl.when(jnp.logical_and(turn >= 0, turn < groups))
        def _():
            relay(turn)

            @pl.when(me == last)
            def _():
                for target in range(last):
                    ready = -(-(target + 1) * share // group_rows) - 1

                    @pl.when(turn == ready)
                    def _():
                        final_copy(target).start()

                @pl.when(turn == groups - 1)
                def _():
                    own_copy().start()

        return 0

    lax.fori_loop(0, groups + max(groups, members), step, 0)

    for group in range(groups):
        out_copy(group).wait()

    @pl.when(me == last)
    def _():
        own_copy().wait()
        for target in range(last):
            final_copy(target).wait_send()

    @pl.when(me < last)
    def _():
        final_copy(0).wait_recv()

        def sent(pair, _):
            state_copy(pair).wait_send()
            return 0

        lax.fori_loop(0, pairs, sent, 0)


def hand_on(out_in, final_in, out, final, rows, turned, out_sem, final_sem):
    T = out.shape[0]
    size = T // PIECES
    arriving = pltpu.make_async_copy(final_in, rows, final_sem.at[0])
    arriving.start()
    pieces = [
        pltpu.make_async_copy(
            out_in.at[pl.ds(i * size, size), :], out.at[pl.ds(i * size, size), :], out_sem.at[i]
        )
        for i in range(PIECES)
    ]
    for piece in pieces:
        piece.start()
    arriving.wait()
    turned[...] = jnp.transpose(rows[...])
    leaving = pltpu.make_async_copy(turned, final, final_sem.at[1])
    leaving.start()
    for piece in pieces:
        piece.wait()
    leaving.wait()


def on_device(r, lf, k, v, e, a, u, g, *, members):
    sequences, T, channels = r.shape
    pairs = channels // LANES
    share = channels // members
    call = pl.pallas_call(
        functools.partial(kernel, members),
        out_shape=(
            jax.ShapeDtypeStruct((T, channels), BF16),
            jax.ShapeDtypeStruct((share, C), F32),
        ),
        in_specs=[pl.BlockSpec(memory_space=pl.ANY)] * 8,
        out_specs=[pl.BlockSpec(memory_space=pl.ANY), pl.BlockSpec(memory_space=pltpu.VMEM)],
        scratch_shapes=[pltpu.VMEM((T, channels), BF16)] * 6
        + [pltpu.VMEM((channels,), F32)] * 2
        + [pltpu.VMEM((T, channels), BF16)]
        + [
            pltpu.VMEM((pairs, T + C, LANES), F32),
            pltpu.VMEM((pairs, T + C, LANES), F32),
            pltpu.VMEM((pairs, C, LANES), F32),
            pltpu.VMEM((pairs, C, LANES), F32),
            pltpu.VMEM((channels, C), F32),
            pltpu.SemaphoreType.DMA((pairs,)),
            pltpu.SemaphoreType.DMA((pairs,)),
            pltpu.SemaphoreType.DMA((members - 1,)),
            pltpu.SemaphoreType.DMA,
            pltpu.SemaphoreType.DMA,
            pltpu.SemaphoreType.DMA((6, pairs // GROUP)),
            pltpu.SemaphoreType.DMA((2,)),
            pltpu.SemaphoreType.DMA((pairs // GROUP,)),
        ],
        compiler_params=pltpu.CompilerParams(
            collective_id=0, has_side_effects=True, vmem_limit_bytes=VMEM_GRANT
        ),
    )
    out, final = call(
        *(x.reshape(T, channels) for x in (r, lf, k, v, e, a)),
        u,
        g,
    )
    out, final = pl.pallas_call(
        hand_on,
        out_shape=(
            jax.ShapeDtypeStruct((T, channels), BF16),
            jax.ShapeDtypeStruct((C, share), F32),
        ),
        in_specs=[pl.BlockSpec(memory_space=pl.ANY)] * 2,
        out_specs=[pl.BlockSpec(memory_space=pl.ANY)] * 2,
        scratch_shapes=[
            pltpu.VMEM((share, C), F32),
            pltpu.VMEM((C, share), F32),
            pltpu.SemaphoreType.DMA((PIECES,)),
            pltpu.SemaphoreType.DMA((2,)),
        ],
        compiler_params=pltpu.CompilerParams(vmem_limit_bytes=VMEM_GRANT),
    )(out, final)
    return out.reshape(sequences, T, channels), jnp.transpose(final).reshape(sequences, share, C)


def solution(mesh):
    split_spec = P(("groups", "dp"), "seq", None)
    return jax.shard_map(
        functools.partial(on_device, members=mesh.shape["seq"]),
        mesh=mesh,
        in_specs=(split_spec,) * 6 + (P(), P()),
        out_specs=(split_spec, split_spec),
        check_vma=False,
    )
```

```python
import functools

import jax
import jax.numpy as jnp
from jax import lax
from jax.experimental import pallas as pl
from jax.experimental.pallas import tpu as pltpu
from jax.sharding import PartitionSpec as P

C = 64
LANES = 128
KEY_EPS = 1e-05
NORM_EPS = 0.00064
FINE_LEVELS = 3
GROUP = 2
PIECES = 4
VMEM_GRANT = 60 * 1024 * 1024
F32 = jnp.float32
BF16 = jnp.bfloat16
MESH = pl.DeviceIdType.MESH


def split(x):
    hi = x.astype(BF16)
    return hi, (x - hi.astype(F32)).astype(BF16)


def dot(a, b):
    return lax.dot_general(a, b, (((1,), (0,)), ((), ())), preferred_element_type=F32)


def dot_t(a, b):
    return lax.dot_general(a, b, (((1,), (1,)), ((), ())), preferred_element_type=F32)


def cat(parts, axis):
    return jnp.concatenate(parts, axis)


def lane_ids(rows):
    return lax.broadcasted_iota(jnp.int32, (rows, LANES), 1)


def head_sum(x, ones2):
    hi, lo = split(x)
    return dot(cat([hi, lo], 1), ones2)


def split_rolled(x):
    hi = x.astype(BF16)
    return hi, pltpu.roll(x - hi.astype(F32), C, 1).astype(BF16)


def head_scores(h, qhi, qlo_r, khi, khi_r, klo):
    q_first = lane_ids(qhi.shape[0]) < C
    k_first = lane_ids(khi.shape[0]) < C
    if h == 1:
        q_first, k_first = jnp.logical_not(q_first), jnp.logical_not(k_first)
    return dot_t(
        cat([jnp.where(q_first, qhi, qlo_r), qhi], 1),
        cat([jnp.where(k_first, khi, khi_r), jnp.where(k_first, klo, jnp.zeros_like(klo))], 1),
    )


def through_solve(left, x, v):
    lhi, llo = split(left)
    xhi, xlo = split(x)
    rhi = cat([xhi, v], 0)
    return dot(cat([lhi, llo, lhi[:, : x.shape[0]]], 1), cat([rhi, rhi, xlo], 0))


def head_ones():
    rows = lax.broadcasted_iota(jnp.int32, (2 * LANES, LANES), 0)
    cols = lax.broadcasted_iota(jnp.int32, (2 * LANES, LANES), 1)
    same = lax.rem(rows, LANES) // C == cols // C
    return jnp.where(same, 1.0, 0.0).astype(BF16)


def diagonal_state(z):
    first = lane_ids(C) < C
    return cat([jnp.where(first, z, 0.0), jnp.where(first, 0.0, z)], 0)


def product3(a, b):
    ahi, alo = split(a)
    bhi, blo = split(b)
    return dot(cat([ahi, alo, ahi], 1), cat([bhi, bhi, blo], 0))


def kernel(
    members,
    r_in, lf_in, k_in, v_in, e_in, a_in, u_in, g_in,
    out_hbm, final_ref,
    r_ref, lf_ref, k_ref, v_ref, e_ref, a_ref, u_ref, g_ref, out_ref,
    reader_buf, sides_buf, x_buf, w_buf, add_buf, z_in, z_out, s_buf,
    send_sem, recv_sem, fsend_sem, frecv_sem, local_sem, in_sem, gain_sem, out_sem,
):
    T, channels = r_ref.shape
    pairs = channels // LANES
    groups = pairs // GROUP
    share = final_ref.shape[0]
    last = members - 1
    me = lax.axis_index("seq")
    barrier = pltpu.get_barrier_semaphore()
    for hop in range(1, members):
        pl.semaphore_signal(
            barrier, inc=1, device_id={"seq": lax.rem(me + hop, members)}, device_id_type=MESH
        )

    arrays = (
        (r_in, r_ref), (lf_in, lf_ref), (k_in, k_ref), (v_in, v_ref), (e_in, e_ref), (a_in, a_ref)
    )

    def input_copies(group):
        at = pl.ds(pl.multiple_of(group * (GROUP * LANES), LANES), GROUP * LANES)
        return [
            pltpu.make_async_copy(source.at[:, at], target.at[:, at], in_sem.at[i, group])
            for i, (source, target) in enumerate(arrays)
        ]

    for group in range(groups):
        for copy in input_copies(group):
            copy.start()
    gain_copies = [
        pltpu.make_async_copy(source, target, gain_sem.at[i])
        for i, (source, target) in enumerate(((u_in, u_ref), (g_in, g_ref)))
    ]
    for copy in gain_copies:
        copy.start()

    @pl.when(me == 0)
    def _():
        z_in[...] = jnp.zeros_like(z_in)

    def lanes_of(pair):
        return pl.ds(pl.multiple_of(pair * LANES, LANES), LANES)

    def compute(group):
        for copy in input_copies(group):
            copy.wait()
        rows = lax.broadcasted_iota(jnp.int32, (T, T), 0)
        cols = lax.broadcasted_iota(jnp.int32, (T, T), 1)
        strict = rows > cols
        lower = jnp.where(rows >= cols, 1.0, 0.0).astype(BF16)
        first = lane_ids(T) < C
        ones2 = head_ones()
        state_lanes = lane_ids(C) < C
        diag = lax.rem(lane_ids(C), C) == lax.broadcasted_iota(jnp.int32, (C, LANES), 0)
        heads = []
        ends = []
        for j in range(GROUP):
            at = lanes_of(group * GROUP + j)
            w = -jnp.exp(lf_ref[:, at].astype(F32))
            whi, wlo = split(w)
            both = dot(lower, cat([whi, wlo], 1))
            cum = both[:, :LANES] + both[:, LANES:]
            mid = cum[T // 2 - 1 : T // 2, :]
            end = cum[T - 1 : T, :]
            c = cum - mid
            e_c = jnp.exp(c)
            e_b = jnp.exp(c - w)
            e_inv = jnp.exp(-c)
            g_mid = jnp.exp(mid)
            g_end = jnp.exp(end - mid)
            gamma = jnp.exp(end)
            e = e_ref[:, at].astype(F32)
            kappa = e * lax.rsqrt(head_sum(e * e, ones2) * (1.0 / C) + KEY_EPS) * C**-0.5
            toward = -kappa * e_b
            reader = r_ref[:, at].astype(F32) * e_c
            away = kappa * a_ref[:, at].astype(F32) * e_inv
            keys = k_ref[:, at].astype(F32) * e_inv
            toward_true = toward * g_mid
            reader_true = reader * g_mid
            away_t = jnp.transpose(away * g_end)
            keys_t = jnp.transpose(keys * g_end)
            vroll = pltpu.roll(v_ref[:, at].astype(F32), C, 1)
            vroll_b = vroll.astype(BF16)
            vroll2 = cat([vroll_b, vroll_b], 0)
            thi, tlo = split_rolled(toward)
            rhi, rlo = split_rolled(reader)
            sides = cat([away, keys], 0)
            khi = sides.astype(BF16)
            klo = (sides - khi.astype(F32)).astype(BF16)
            khi_r = pltpu.roll(khi.astype(F32), C, 1).astype(BF16)
            pair = group * GROUP + j
            reader_buf[pair, 0] = rhi
            reader_buf[pair, 1] = rlo
            sides_buf[pair, 0] = khi
            sides_buf[pair, 1] = khi_r
            sides_buf[pair, 2] = klo
            w_buf[pair, :T, :] = reader_true
            ends.append(jnp.where(diag, gamma, 0.0))
            for h in range(2):
                own = first if h == 0 else jnp.logical_not(first)
                scores = head_scores(h, thi, tlo, khi, khi_r, klo)
                mix_away = jnp.where(strict, scores[:, :T], 0.0)
                mix_keys = jnp.where(strict, scores[:, T:], 0.0)
                mhi, mlo = split(mix_keys)
                mixed = dot(cat([mhi, mlo], 1), vroll2)
                heads.append(
                    dict(
                        y=mix_away,
                        x=jnp.where(own, toward_true, mixed),
                        left=cat([away_t[h * C : h * C + C], keys_t[h * C : h * C + C]], 1),
                        v=jnp.where(own, 0.0, vroll).astype(BF16),
                    )
                )
        levels = (T - 1).bit_length()
        for level in range(levels):
            fine = level < FINE_LEVELS
            skip = 2**level if 2**level >= 16 else 0
            later = 2 ** (level + 1) if 2 ** (level + 1) >= 16 else 0
            for head in heads:
                y, x = head["y"], head["x"]
                if fine:
                    yhi, ylo = split(y)
                    rhi, rlo = split(cat([y, x], 1))
                    prod = dot(cat([yhi, ylo, yhi], 1), cat([rhi, rhi, rlo], 0))
                else:
                    y, right = y.astype(BF16), x.astype(BF16)
                    if level < levels - 1:
                        full = cat([jnp.zeros((skip, T), BF16), y], 0) if skip else y
                        right = cat([full, right], 1)
                    prod = dot(y, right)
                if level < levels - 1:
                    head["y"] = prod[later - skip :, :T]
                gained = prod[:, -LANES:]
                head["x"] = cat([x[:skip], x[skip:] + gained], 0) if skip else x + gained
        for j in range(GROUP):
            pair = group * GROUP + j
            results = []
            for h, head in enumerate(heads[2 * j : 2 * j + 2]):
                x_buf[pair, h] = head["x"]
                results.append(through_solve(head["left"], head["x"], head["v"]))
            w_buf[pair, T:, :] = jnp.where(state_lanes, results[0], results[1]) + ends[j]
            add_buf[pair, T:, :] = pltpu.roll(
                jnp.where(state_lanes, results[1], results[0]), C, 1
            )

    def read(group):
        rows = lax.broadcasted_iota(jnp.int32, (T, 2 * T), 0)
        cols = lax.rem(lax.broadcasted_iota(jnp.int32, (T, 2 * T), 1), T)
        inclusive = rows >= cols
        first = lane_ids(T) < C
        for j in range(GROUP):
            pair = group * GROUP + j
            vroll = pltpu.roll(v_ref[:, lanes_of(pair)].astype(F32), C, 1)
            results = []
            for h in range(2):
                own = first if h == 0 else jnp.logical_not(first)
                scores = head_scores(
                    h, reader_buf[pair, 0], reader_buf[pair, 1],
                    sides_buf[pair, 0], sides_buf[pair, 1], sides_buf[pair, 2],
                )
                own_v = jnp.where(own, 0.0, vroll).astype(BF16)
                left = jnp.where(inclusive, scores, 0.0)
                results.append(through_solve(left, x_buf[pair, h], own_v))
            w_buf[pair, :T, :] += jnp.where(first, results[0], results[1])
            add_buf[pair, :T, :] = pltpu.roll(jnp.where(first, results[1], results[0]), C, 1)

    def state_copy(pair):
        return pltpu.make_async_remote_copy(
            src_ref=z_out.at[pair],
            dst_ref=z_in.at[pair],
            send_sem=send_sem.at[pair],
            recv_sem=recv_sem.at[pair],
            device_id={"seq": lax.rem(me + 1, members)},
            device_id_type=MESH,
        )

    def relay(group):
        for j in range(GROUP):
            pair = group * GROUP + j

            @pl.when(me == 0)
            def _():
                z_out[pair] = add_buf[pair, T:, :]

            @pl.when(me > 0)
            def _():
                state_copy(pair).wait_recv()
                z = diagonal_state(z_in[pair])
                z_out[pair] = product3(w_buf[pair, T:, :], z) + add_buf[pair, T:, :]

            @pl.when(me < last)
            def _():
                state_copy(pair).start()

            @pl.when(me == last)
            def _():
                s_buf[pl.ds(pl.multiple_of(pair * LANES, LANES), LANES), :] = jnp.transpose(
                    z_out[pair]
                )

    def out_copy(group):
        at = pl.ds(pl.multiple_of(group * (GROUP * LANES), LANES), GROUP * LANES)
        return pltpu.make_async_copy(out_ref.at[:, at], out_hbm.at[:, at], out_sem.at[group])

    def finish(group):
        ones2 = head_ones()
        for j in range(GROUP):
            pair = group * GROUP + j
            at = lanes_of(pair)
            z = diagonal_state(z_in[pair])
            result = product3(w_buf[pair, :T, :], z) + add_buf[pair, :T, :]
            average = head_sum(result, ones2) * (1.0 / C)
            centered = result - average
            spread = head_sum(centered * centered, ones2) * (1.0 / C)
            normed = centered * lax.rsqrt(spread + NORM_EPS) * g_ref[at][None, :]
            bonus = r_ref[:, at].astype(F32) * k_ref[:, at].astype(F32) * u_ref[at][None, :]
            extra = head_sum(bonus, ones2) * v_ref[:, at].astype(F32)
            out_ref[:, at] = (normed + extra).astype(out_ref.dtype)
        out_copy(group).start()

    def final_copy(target):
        return pltpu.make_async_remote_copy(
            src_ref=s_buf.at[pl.ds(pl.multiple_of(target * share, 8), share), :],
            dst_ref=final_ref,
            send_sem=fsend_sem.at[target],
            recv_sem=frecv_sem,
            device_id={"seq": target},
            device_id_type=MESH,
        )

    def own_copy():
        return pltpu.make_async_copy(s_buf.at[pl.ds(last * share, share), :], final_ref, local_sem)

    group_rows = GROUP * LANES
    read_from = groups - (me // last) * (groups - 1)
    finish_from = jnp.maximum(me, read_from)

    def step(s, _):
        @pl.when(s < groups)
        def _():
            compute(s)

        @pl.when(s == 0)
        def _():
            pl.semaphore_wait(barrier, members - 1)
            for copy in gain_copies:
                copy.wait()

        turn = s - me

        @pl.when(jnp.logical_and(turn >= 0, turn < groups))
        def _():
            relay(turn)

            @pl.when(me == last)
            def _():
                for target in range(last):
                    ready = -(-(target + 1) * share // group_rows) - 1

                    @pl.when(turn == ready)
                    def _():
                        final_copy(target).start()

                @pl.when(turn == groups - 1)
                def _():
                    own_copy().start()

        ahead = s - read_from

        @pl.when(jnp.logical_and(ahead >= 0, ahead < groups))
        def _():
            read(ahead)

        done = s - finish_from

        @pl.when(jnp.logical_and(done >= 0, done < groups))
        def _():
            finish(done)

        return 0

    lax.fori_loop(0, groups + max(groups, members), step, 0)

    for group in range(groups):
        out_copy(group).wait()

    @pl.when(me == last)
    def _():
        own_copy().wait()
        for target in range(last):
            final_copy(target).wait_send()

    @pl.when(me < last)
    def _():
        final_copy(0).wait_recv()

        def sent(pair, _):
            state_copy(pair).wait_send()
            return 0

        lax.fori_loop(0, pairs, sent, 0)


def hand_on(out_in, final_in, out, final, rows, turned, held, in_sem, out_sem, final_sem):
    T = out.shape[0]
    size = T // PIECES
    arriving = pltpu.make_async_copy(final_in, rows, final_sem.at[0])
    arriving.start()
    parts = [pl.ds(i * size, size) for i in range(PIECES)]
    loads = [
        pltpu.make_async_copy(out_in.at[at, :], held.at[at, :], in_sem.at[i])
        for i, at in enumerate(parts)
    ]
    stores = [
        pltpu.make_async_copy(held.at[at, :], out.at[at, :], out_sem.at[i])
        for i, at in enumerate(parts)
    ]
    for load in loads:
        load.start()
    arriving.wait()
    turned[...] = jnp.transpose(rows[...])
    leaving = pltpu.make_async_copy(turned, final, final_sem.at[1])
    leaving.start()
    for load, store in zip(loads, stores):
        load.wait()
        store.start()
    for store in stores:
        store.wait()
    leaving.wait()


def on_device(r, lf, k, v, e, a, u, g, *, members):
    sequences, T, channels = r.shape
    pairs = channels // LANES
    share = channels // members
    call = pl.pallas_call(
        functools.partial(kernel, members),
        out_shape=(
            jax.ShapeDtypeStruct((T, channels), BF16),
            jax.ShapeDtypeStruct((share, C), F32),
        ),
        in_specs=[pl.BlockSpec(memory_space=pl.ANY)] * 8,
        out_specs=[pl.BlockSpec(memory_space=pl.ANY), pl.BlockSpec(memory_space=pltpu.VMEM)],
        scratch_shapes=[pltpu.VMEM((T, channels), BF16)] * 6
        + [pltpu.VMEM((channels,), F32)] * 2
        + [pltpu.VMEM((T, channels), BF16)]
        + [
            pltpu.VMEM((pairs, 2, T, LANES), BF16),
            pltpu.VMEM((pairs, 3, 2 * T, LANES), BF16),
            pltpu.VMEM((pairs, 2, T, LANES), F32),
            pltpu.VMEM((pairs, T + C, LANES), F32),
            pltpu.VMEM((pairs, T + C, LANES), F32),
            pltpu.VMEM((pairs, C, LANES), F32),
            pltpu.VMEM((pairs, C, LANES), F32),
            pltpu.VMEM((channels, C), F32),
            pltpu.SemaphoreType.DMA((pairs,)),
            pltpu.SemaphoreType.DMA((pairs,)),
            pltpu.SemaphoreType.DMA((members - 1,)),
            pltpu.SemaphoreType.DMA,
            pltpu.SemaphoreType.DMA,
            pltpu.SemaphoreType.DMA((6, pairs // GROUP)),
            pltpu.SemaphoreType.DMA((2,)),
            pltpu.SemaphoreType.DMA((pairs // GROUP,)),
        ],
        compiler_params=pltpu.CompilerParams(
            collective_id=0, has_side_effects=True, vmem_limit_bytes=VMEM_GRANT
        ),
    )
    out, final = call(
        *(x.reshape(T, channels) for x in (r, lf, k, v, e, a)),
        u,
        g,
    )
    out, final = pl.pallas_call(
        hand_on,
        out_shape=(
            jax.ShapeDtypeStruct((T, channels), BF16),
            jax.ShapeDtypeStruct((C, share), F32),
        ),
        in_specs=[pl.BlockSpec(memory_space=pl.ANY)] * 2,
        out_specs=[pl.BlockSpec(memory_space=pl.ANY)] * 2,
        scratch_shapes=[
            pltpu.VMEM((share, C), F32),
            pltpu.VMEM((C, share), F32),
            pltpu.VMEM((T, channels), BF16),
            pltpu.SemaphoreType.DMA((PIECES,)),
            pltpu.SemaphoreType.DMA((PIECES,)),
            pltpu.SemaphoreType.DMA((2,)),
        ],
        compiler_params=pltpu.CompilerParams(vmem_limit_bytes=VMEM_GRANT),
    )(out, final)
    return out.reshape(sequences, T, channels), jnp.transpose(final).reshape(sequences, share, C)


def solution(mesh):
    split_spec = P(("groups", "dp"), "seq", None)
    return jax.shard_map(
        functools.partial(on_device, members=mesh.shape["seq"]),
        mesh=mesh,
        in_specs=(split_spec,) * 6 + (P(), P()),
        out_specs=(split_spec, split_spec),
        check_vma=False,
    )
```

```python
import functools

import jax
import jax.numpy as jnp
from jax import lax
from jax.experimental import pallas as pl
from jax.experimental.pallas import tpu as pltpu
from jax.sharding import PartitionSpec as P

C = 64
LANES = 128
KEY_EPS = 1e-05
NORM_EPS = 0.00064
FINE_LEVELS = 3
GROUP = 2
PIECES = 4
VMEM_GRANT = 60 * 1024 * 1024
F32 = jnp.float32
BF16 = jnp.bfloat16
MESH = pl.DeviceIdType.MESH


def split(x):
    hi = x.astype(BF16)
    return hi, (x - hi.astype(F32)).astype(BF16)


def dot(a, b):
    return lax.dot_general(a, b, (((1,), (0,)), ((), ())), preferred_element_type=F32)


def dot_t(a, b):
    return lax.dot_general(a, b, (((1,), (1,)), ((), ())), preferred_element_type=F32)


def cat(parts, axis):
    return jnp.concatenate(parts, axis)


def lane_ids(rows):
    return lax.broadcasted_iota(jnp.int32, (rows, LANES), 1)


def head_sum(x, ones2):
    hi, lo = split(x)
    return dot(cat([hi, lo], 1), ones2)


def head_ones():
    rows = lax.broadcasted_iota(jnp.int32, (2 * LANES, LANES), 0)
    cols = lax.broadcasted_iota(jnp.int32, (2 * LANES, LANES), 1)
    same = lax.rem(rows, LANES) // C == cols // C
    return jnp.where(same, 1.0, 0.0).astype(BF16)


def diagonal_state(z):
    first = lane_ids(C) < C
    return cat([jnp.where(first, z, 0.0), jnp.where(first, 0.0, z)], 0)


def product3(a, b):
    ahi, alo = split(a)
    bhi, blo = split(b)
    return dot(cat([ahi, alo, ahi], 1), cat([bhi, bhi, blo], 0))


def kernel(
    members,
    r_in, lf_in, k_in, v_in, e_in, a_in, u_in, g_in,
    out_hbm, final_ref,
    r_ref, lf_ref, k_ref, v_ref, e_ref, a_ref, u_ref, g_ref, out_ref,
    w_buf, add_buf, z_in, z_out, s_buf,
    send_sem, recv_sem, fsend_sem, frecv_sem, local_sem, in_sem, gain_sem, out_sem,
):
    T, channels = r_ref.shape
    pairs = channels // LANES
    groups = pairs // GROUP
    share = final_ref.shape[0]
    last = members - 1
    me = lax.axis_index("seq")
    barrier = pltpu.get_barrier_semaphore()
    for hop in range(1, members):
        pl.semaphore_signal(
            barrier, inc=1, device_id={"seq": lax.rem(me + hop, members)}, device_id_type=MESH
        )

    arrays = (
        (r_in, r_ref), (lf_in, lf_ref), (k_in, k_ref), (v_in, v_ref), (e_in, e_ref), (a_in, a_ref)
    )

    def input_copies(group):
        at = pl.ds(pl.multiple_of(group * (GROUP * LANES), LANES), GROUP * LANES)
        return [
            pltpu.make_async_copy(source.at[:, at], target.at[:, at], in_sem.at[i, group])
            for i, (source, target) in enumerate(arrays)
        ]

    for group in range(groups):
        for copy in input_copies(group):
            copy.start()
    gain_copies = [
        pltpu.make_async_copy(source, target, gain_sem.at[i])
        for i, (source, target) in enumerate(((u_in, u_ref), (g_in, g_ref)))
    ]
    for copy in gain_copies:
        copy.start()

    @pl.when(me == 0)
    def _():
        z_in[...] = jnp.zeros_like(z_in)

    def lanes_of(pair):
        return pl.ds(pl.multiple_of(pair * LANES, LANES), LANES)

    def compute(group):
        for copy in input_copies(group):
            copy.wait()
        rows = lax.broadcasted_iota(jnp.int32, (T, T), 0)
        cols = lax.broadcasted_iota(jnp.int32, (T, T), 1)
        inclusive = rows >= cols
        strict = rows > cols
        lower = jnp.where(inclusive, 1.0, 0.0).astype(BF16)
        first = lane_ids(T) < C
        ones2 = head_ones()
        state_lanes = lane_ids(T + C) < C
        diag = lax.rem(lane_ids(C), C) == lax.broadcasted_iota(jnp.int32, (C, LANES), 0)
        heads = []
        ends = []
        for j in range(GROUP):
            at = lanes_of(group * GROUP + j)
            w = -jnp.exp(lf_ref[:, at].astype(F32))
            whi, wlo = split(w)
            both = dot(lower, cat([whi, wlo], 1))
            cum = both[:, :LANES] + both[:, LANES:]
            mid = cum[T // 2 - 1 : T // 2, :]
            end = cum[T - 1 : T, :]
            c = cum - mid
            e_c = jnp.exp(c)
            e_b = jnp.exp(c - w)
            e_inv = jnp.exp(-c)
            g_mid = jnp.exp(mid)
            g_end = jnp.exp(end - mid)
            gamma = jnp.exp(end)
            e = e_ref[:, at].astype(F32)
            kappa = e * lax.rsqrt(head_sum(e * e, ones2) * (1.0 / C) + KEY_EPS) * C**-0.5
            toward = -kappa * e_b
            reader = r_ref[:, at].astype(F32) * e_c
            away = kappa * a_ref[:, at].astype(F32) * e_inv
            keys = k_ref[:, at].astype(F32) * e_inv
            toward_true = toward * g_mid
            reader_true = reader * g_mid
            away_t = jnp.transpose(away * g_end)
            keys_t = jnp.transpose(keys * g_end)
            vroll = pltpu.roll(v_ref[:, at].astype(F32), C, 1)
            vroll_b = vroll.astype(BF16)
            vroll2 = cat([vroll_b, vroll_b], 0)
            first2 = lane_ids(2 * T) < C
            query = cat([toward, reader], 0)
            qhi = query.astype(BF16)
            qlo_r = pltpu.roll(query - qhi.astype(F32), C, 1).astype(BF16)
            sides = cat([away, keys], 0)
            khi = sides.astype(BF16)
            klo = (sides - khi.astype(F32)).astype(BF16)
            khi_r = pltpu.roll(khi.astype(F32), C, 1).astype(BF16)
            ends.append((reader_true, jnp.where(diag, gamma, 0.0)))
            for h in range(2):
                own = first if h == 0 else jnp.logical_not(first)
                own2 = first2 if h == 0 else jnp.logical_not(first2)
                scores = dot_t(
                    cat([jnp.where(own2, qhi, qlo_r), qhi], 1),
                    cat([jnp.where(own2, khi, khi_r), jnp.where(own2, klo, jnp.zeros_like(klo))], 1),
                )
                mix_away = jnp.where(strict, scores[:T, :T], 0.0)
                mix_keys = jnp.where(strict, scores[:T, T:], 0.0)
                read = cat(
                    [
                        jnp.where(inclusive, scores[T:, :T], 0.0),
                        jnp.where(inclusive, scores[T:, T:], 0.0),
                    ],
                    1,
                )
                closing = cat([away_t[h * C : h * C + C], keys_t[h * C : h * C + C]], 1)
                mhi, mlo = split(mix_keys)
                mixed = dot(cat([mhi, mlo], 1), vroll2)
                heads.append(
                    dict(
                        y=mix_away,
                        x=jnp.where(own, toward_true, mixed),
                        left=cat([read, closing], 0),
                        v=jnp.where(own, 0.0, vroll).astype(BF16),
                    )
                )
        levels = (T - 1).bit_length()
        for level in range(levels):
            fine = level < FINE_LEVELS
            skip = 2**level if 2**level >= 16 else 0
            later = 2 ** (level + 1) if 2 ** (level + 1) >= 16 else 0
            for head in heads:
                y, x = head["y"], head["x"]
                if fine:
                    yhi, ylo = split(y)
                    rhi, rlo = split(cat([y, x], 1))
                    prod = dot(cat([yhi, ylo, yhi], 1), cat([rhi, rhi, rlo], 0))
                else:
                    y, right = y.astype(BF16), x.astype(BF16)
                    if level < levels - 1:
                        full = cat([jnp.zeros((skip, T), BF16), y], 0) if skip else y
                        right = cat([full, right], 1)
                    prod = dot(y, right)
                if level < levels - 1:
                    head["y"] = prod[later - skip :, :T]
                gained = prod[:, -LANES:]
                head["x"] = cat([x[:skip], x[skip:] + gained], 0) if skip else x + gained
        for j in range(GROUP):
            results = []
            for head in heads[2 * j : 2 * j + 2]:
                lhi, llo = split(head["left"])
                xhi, xlo = split(head["x"])
                rhi = cat([xhi, head["v"]], 0)
                results.append(dot(cat([lhi, llo, lhi[:, :T]], 1), cat([rhi, rhi, xlo], 0)))
            pair = group * GROUP + j
            w_buf[pair] = jnp.where(state_lanes, results[0], results[1]) + cat(list(ends[j]), 0)
            add_buf[pair] = pltpu.roll(jnp.where(state_lanes, results[1], results[0]), C, 1)

    def state_copy(pair):
        return pltpu.make_async_remote_copy(
            src_ref=z_out.at[pair],
            dst_ref=z_in.at[pair],
            send_sem=send_sem.at[pair],
            recv_sem=recv_sem.at[pair],
            device_id={"seq": lax.rem(me + 1, members)},
            device_id_type=MESH,
        )

    def relay(group):
        for j in range(GROUP):
            pair = group * GROUP + j

            @pl.when(me == 0)
            def _():
                z_out[pair] = add_buf[pair, T:, :]

            @pl.when(me > 0)
            def _():
                state_copy(pair).wait_recv()
                z = diagonal_state(z_in[pair])
                z_out[pair] = product3(w_buf[pair, T:, :], z) + add_buf[pair, T:, :]

            @pl.when(me < last)
            def _():
                state_copy(pair).start()

            @pl.when(me == last)
            def _():
                s_buf[pl.ds(pl.multiple_of(pair * LANES, LANES), LANES), :] = jnp.transpose(
                    z_out[pair]
                )

    def out_copy(group):
        at = pl.ds(pl.multiple_of(group * (GROUP * LANES), LANES), GROUP * LANES)
        return pltpu.make_async_copy(out_ref.at[:, at], out_hbm.at[:, at], out_sem.at[group])

    def finish(group):
        ones2 = head_ones()
        for j in range(GROUP):
            pair = group * GROUP + j
            at = lanes_of(pair)
            z = diagonal_state(z_in[pair])
            result = product3(w_buf[pair, :T, :], z) + add_buf[pair, :T, :]
            average = head_sum(result, ones2) * (1.0 / C)
            centered = result - average
            spread = head_sum(centered * centered, ones2) * (1.0 / C)
            normed = centered * lax.rsqrt(spread + NORM_EPS) * g_ref[at][None, :]
            bonus = r_ref[:, at].astype(F32) * k_ref[:, at].astype(F32) * u_ref[at][None, :]
            extra = head_sum(bonus, ones2) * v_ref[:, at].astype(F32)
            out_ref[:, at] = (normed + extra).astype(out_ref.dtype)
        out_copy(group).start()

    def final_copy(target):
        return pltpu.make_async_remote_copy(
            src_ref=s_buf.at[pl.ds(pl.multiple_of(target * share, 8), share), :],
            dst_ref=final_ref,
            send_sem=fsend_sem.at[target],
            recv_sem=frecv_sem,
            device_id={"seq": target},
            device_id_type=MESH,
        )

    def own_copy():
        return pltpu.make_async_copy(s_buf.at[pl.ds(last * share, share), :], final_ref, local_sem)

    group_rows = GROUP * LANES
    finish_from = jnp.maximum(me + 1, groups - (me // last) * groups)

    def step(s, _):
        @pl.when(s < groups)
        def _():
            compute(s)

        @pl.when(s == 0)
        def _():
            pl.semaphore_wait(barrier, members - 1)
            for copy in gain_copies:
                copy.wait()

        done = s - finish_from

        @pl.when(jnp.logical_and(done >= 0, done < groups))
        def _():
            finish(done)

        turn = s - me

        @pl.when(jnp.logical_and(turn >= 0, turn < groups))
        def _():
            relay(turn)

            @pl.when(me == last)
            def _():
                for target in range(last):
                    ready = -(-(target + 1) * share // group_rows) - 1

                    @pl.when(turn == ready)
                    def _():
                        final_copy(target).start()

                @pl.when(turn == groups - 1)
                def _():
                    own_copy().start()

        return 0

    lax.fori_loop(0, groups + max(groups, members), step, 0)

    for group in range(groups):
        out_copy(group).wait()

    @pl.when(me == last)
    def _():
        own_copy().wait()
        for target in range(last):
            final_copy(target).wait_send()

    @pl.when(me < last)
    def _():
        final_copy(0).wait_recv()

        def sent(pair, _):
            state_copy(pair).wait_send()
            return 0

        lax.fori_loop(0, pairs, sent, 0)


def hand_on(out_in, final_in, out, final, rows, turned, held, in_sem, out_sem, final_sem):
    T = out.shape[0]
    size = T // PIECES
    arriving = pltpu.make_async_copy(final_in, rows, final_sem.at[0])
    arriving.start()
    parts = [pl.ds(i * size, size) for i in range(PIECES)]
    loads = [
        pltpu.make_async_copy(out_in.at[at, :], held.at[at, :], in_sem.at[i])
        for i, at in enumerate(parts)
    ]
    stores = [
        pltpu.make_async_copy(held.at[at, :], out.at[at, :], out_sem.at[i])
        for i, at in enumerate(parts)
    ]
    for load in loads:
        load.start()
    arriving.wait()
    turned[...] = jnp.transpose(rows[...])
    leaving = pltpu.make_async_copy(turned, final, final_sem.at[1])
    leaving.start()
    for load, store in zip(loads, stores):
        load.wait()
        store.start()
    for store in stores:
        store.wait()
    leaving.wait()


def on_device(r, lf, k, v, e, a, u, g, *, members):
    sequences, T, channels = r.shape
    pairs = channels // LANES
    share = channels // members
    call = pl.pallas_call(
        functools.partial(kernel, members),
        out_shape=(
            jax.ShapeDtypeStruct((T, channels), BF16),
            jax.ShapeDtypeStruct((share, C), F32),
        ),
        in_specs=[pl.BlockSpec(memory_space=pl.ANY)] * 8,
        out_specs=[pl.BlockSpec(memory_space=pl.ANY), pl.BlockSpec(memory_space=pltpu.VMEM)],
        scratch_shapes=[pltpu.VMEM((T, channels), BF16)] * 6
        + [pltpu.VMEM((channels,), F32)] * 2
        + [pltpu.VMEM((T, channels), BF16)]
        + [
            pltpu.VMEM((pairs, T + C, LANES), F32),
            pltpu.VMEM((pairs, T + C, LANES), F32),
            pltpu.VMEM((pairs, C, LANES), F32),
            pltpu.VMEM((pairs, C, LANES), F32),
            pltpu.VMEM((channels, C), F32),
            pltpu.SemaphoreType.DMA((pairs,)),
            pltpu.SemaphoreType.DMA((pairs,)),
            pltpu.SemaphoreType.DMA((members - 1,)),
            pltpu.SemaphoreType.DMA,
            pltpu.SemaphoreType.DMA,
            pltpu.SemaphoreType.DMA((6, pairs // GROUP)),
            pltpu.SemaphoreType.DMA((2,)),
            pltpu.SemaphoreType.DMA((pairs // GROUP,)),
        ],
        compiler_params=pltpu.CompilerParams(
            collective_id=0, has_side_effects=True, vmem_limit_bytes=VMEM_GRANT
        ),
    )
    out, final = call(
        *(x.reshape(T, channels) for x in (r, lf, k, v, e, a)),
        u,
        g,
    )
    out, final = pl.pallas_call(
        hand_on,
        out_shape=(
            jax.ShapeDtypeStruct((T, channels), BF16),
            jax.ShapeDtypeStruct((C, share), F32),
        ),
        in_specs=[pl.BlockSpec(memory_space=pl.ANY)] * 2,
        out_specs=[pl.BlockSpec(memory_space=pl.ANY)] * 2,
        scratch_shapes=[
            pltpu.VMEM((share, C), F32),
            pltpu.VMEM((C, share), F32),
            pltpu.VMEM((T, channels), BF16),
            pltpu.SemaphoreType.DMA((PIECES,)),
            pltpu.SemaphoreType.DMA((PIECES,)),
            pltpu.SemaphoreType.DMA((2,)),
        ],
        compiler_params=pltpu.CompilerParams(vmem_limit_bytes=VMEM_GRANT),
    )(out, final)
    return out.reshape(sequences, T, channels), jnp.transpose(final).reshape(sequences, share, C)


def solution(mesh):
    split_spec = P(("groups", "dp"), "seq", None)
    return jax.shard_map(
        functools.partial(on_device, members=mesh.shape["seq"]),
        mesh=mesh,
        in_specs=(split_spec,) * 6 + (P(), P()),
        out_specs=(split_spec, split_spec),
        check_vma=False,
    )
```

```python
import functools

import jax
import jax.numpy as jnp
from jax import lax
from jax.experimental import pallas as pl
from jax.experimental.pallas import tpu as pltpu
from jax.sharding import PartitionSpec as P

C = 64
LANES = 128
KEY_EPS = 1e-05
NORM_EPS = 0.00064
FINE_LEVELS = 3
GROUP = 2
PIECES = 4
VMEM_GRANT = 60 * 1024 * 1024
F32 = jnp.float32
BF16 = jnp.bfloat16
MESH = pl.DeviceIdType.MESH


def split(x):
    hi = x.astype(BF16)
    return hi, (x - hi.astype(F32)).astype(BF16)


def dot(a, b):
    return lax.dot_general(a, b, (((1,), (0,)), ((), ())), preferred_element_type=F32)


def dot_t(a, b):
    return lax.dot_general(a, b, (((1,), (1,)), ((), ())), preferred_element_type=F32)


def cat(parts, axis):
    return jnp.concatenate(parts, axis)


def lane_ids(rows):
    return lax.broadcasted_iota(jnp.int32, (rows, LANES), 1)


def head_sum(x, ones2):
    hi, lo = split(x)
    return dot(cat([hi, lo], 1), ones2)


def head_ones():
    rows = lax.broadcasted_iota(jnp.int32, (2 * LANES, LANES), 0)
    cols = lax.broadcasted_iota(jnp.int32, (2 * LANES, LANES), 1)
    same = lax.rem(rows, LANES) // C == cols // C
    return jnp.where(same, 1.0, 0.0).astype(BF16)


def diagonal_state(z):
    first = lane_ids(C) < C
    return cat([jnp.where(first, z, 0.0), jnp.where(first, 0.0, z)], 0)


def product3(a, b):
    ahi, alo = split(a)
    bhi, blo = split(b)
    return dot(cat([ahi, alo, ahi], 1), cat([bhi, bhi, blo], 0))


def kernel(
    members,
    r_in, lf_in, k_in, v_in, e_in, a_in, u_in, g_in,
    out_hbm, final_ref,
    r_ref, lf_ref, k_ref, v_ref, e_ref, a_ref, u_ref, g_ref, out_ref,
    w_buf, add_buf, z_in, z_out, s_buf,
    send_sem, recv_sem, fsend_sem, frecv_sem, local_sem, in_sem, gain_sem, out_sem,
):
    T, channels = r_ref.shape
    pairs = channels // LANES
    groups = pairs // GROUP
    share = final_ref.shape[0]
    last = members - 1
    me = lax.axis_index("seq")
    barrier = pltpu.get_barrier_semaphore()
    for hop in range(1, members):
        pl.semaphore_signal(
            barrier, inc=1, device_id={"seq": lax.rem(me + hop, members)}, device_id_type=MESH
        )

    arrays = (
        (r_in, r_ref), (lf_in, lf_ref), (k_in, k_ref), (v_in, v_ref), (e_in, e_ref), (a_in, a_ref)
    )

    def input_copies(group):
        at = pl.ds(pl.multiple_of(group * (GROUP * LANES), LANES), GROUP * LANES)
        return [
            pltpu.make_async_copy(source.at[:, at], target.at[:, at], in_sem.at[i, group])
            for i, (source, target) in enumerate(arrays)
        ]

    for group in range(groups):
        for copy in input_copies(group):
            copy.start()
    gain_copies = [
        pltpu.make_async_copy(source, target, gain_sem.at[i])
        for i, (source, target) in enumerate(((u_in, u_ref), (g_in, g_ref)))
    ]
    for copy in gain_copies:
        copy.start()

    @pl.when(me == 0)
    def _():
        z_in[...] = jnp.zeros_like(z_in)

    def lanes_of(pair):
        return pl.ds(pl.multiple_of(pair * LANES, LANES), LANES)

    def compute(group):
        for copy in input_copies(group):
            copy.wait()
        rows = lax.broadcasted_iota(jnp.int32, (T, T), 0)
        cols = lax.broadcasted_iota(jnp.int32, (T, T), 1)
        inclusive = rows >= cols
        strict = rows > cols
        lower = jnp.where(inclusive, 1.0, 0.0).astype(BF16)
        first = lane_ids(T) < C
        ones2 = head_ones()
        state_lanes = lane_ids(T + C) < C
        diag = lax.rem(lane_ids(C), C) == lax.broadcasted_iota(jnp.int32, (C, LANES), 0)
        heads = []
        ends = []
        for j in range(GROUP):
            at = lanes_of(group * GROUP + j)
            w = -jnp.exp(lf_ref[:, at].astype(F32))
            whi, wlo = split(w)
            both = dot(lower, cat([whi, wlo], 1))
            cum = both[:, :LANES] + both[:, LANES:]
            mid = cum[T // 2 - 1 : T // 2, :]
            end = cum[T - 1 : T, :]
            c = cum - mid
            e_c = jnp.exp(c)
            e_b = jnp.exp(c - w)
            e_inv = jnp.exp(-c)
            g_mid = jnp.exp(mid)
            g_end = jnp.exp(end - mid)
            gamma = jnp.exp(end)
            e = e_ref[:, at].astype(F32)
            kappa = e * lax.rsqrt(head_sum(e * e, ones2) * (1.0 / C) + KEY_EPS) * C**-0.5
            toward = -kappa * e_b
            reader = r_ref[:, at].astype(F32) * e_c
            away = kappa * a_ref[:, at].astype(F32) * e_inv
            keys = k_ref[:, at].astype(F32) * e_inv
            toward_true = toward * g_mid
            reader_true = reader * g_mid
            away_t = jnp.transpose(away * g_end)
            keys_t = jnp.transpose(keys * g_end)
            vroll = pltpu.roll(v_ref[:, at].astype(F32), C, 1)
            vroll_b = vroll.astype(BF16)
            vroll2 = cat([vroll_b, vroll_b], 0)
            first2 = lane_ids(2 * T) < C
            query = cat([toward, reader], 0)
            qhi = query.astype(BF16)
            qlo_r = pltpu.roll(query - qhi.astype(F32), C, 1).astype(BF16)
            sides = cat([away, keys], 0)
            khi = sides.astype(BF16)
            klo = (sides - khi.astype(F32)).astype(BF16)
            khi_r = pltpu.roll(khi.astype(F32), C, 1).astype(BF16)
            ends.append((reader_true, jnp.where(diag, gamma, 0.0)))
            for h in range(2):
                own = first if h == 0 else jnp.logical_not(first)
                own2 = first2 if h == 0 else jnp.logical_not(first2)
                scores = dot_t(
                    cat([jnp.where(own2, qhi, qlo_r), qhi], 1),
                    cat([jnp.where(own2, khi, khi_r), jnp.where(own2, klo, jnp.zeros_like(klo))], 1),
                )
                mix_away = jnp.where(strict, scores[:T, :T], 0.0)
                mix_keys = jnp.where(strict, scores[:T, T:], 0.0)
                read = cat(
                    [
                        jnp.where(inclusive, scores[T:, :T], 0.0),
                        jnp.where(inclusive, scores[T:, T:], 0.0),
                    ],
                    1,
                )
                closing = cat([away_t[h * C : h * C + C], keys_t[h * C : h * C + C]], 1)
                mhi, mlo = split(mix_keys)
                mixed = dot(cat([mhi, mlo], 1), vroll2)
                heads.append(
                    dict(
                        y=mix_away,
                        x=jnp.where(own, toward_true, mixed),
                        left=cat([read, closing], 0),
                        v=jnp.where(own, 0.0, vroll).astype(BF16),
                    )
                )
        levels = (T - 1).bit_length()
        for level in range(levels):
            fine = level < FINE_LEVELS
            skip = 2**level if 2**level >= 16 else 0
            later = 2 ** (level + 1) if 2 ** (level + 1) >= 16 else 0
            for head in heads:
                y, x = head["y"], head["x"]
                if fine:
                    yhi, ylo = split(y)
                    rhi, rlo = split(cat([y, x], 1))
                    prod = dot(cat([yhi, ylo, yhi], 1), cat([rhi, rhi, rlo], 0))
                else:
                    y, right = y.astype(BF16), x.astype(BF16)
                    if level < levels - 1:
                        full = cat([jnp.zeros((skip, T), BF16), y], 0) if skip else y
                        right = cat([full, right], 1)
                    prod = dot(y, right)
                if level < levels - 1:
                    head["y"] = prod[later - skip :, :T]
                gained = prod[:, -LANES:]
                head["x"] = cat([x[:skip], x[skip:] + gained], 0) if skip else x + gained
        for j in range(GROUP):
            results = []
            for head in heads[2 * j : 2 * j + 2]:
                lhi, llo = split(head["left"])
                xhi, xlo = split(head["x"])
                rhi = cat([xhi, head["v"]], 0)
                results.append(dot(cat([lhi, llo, lhi[:, :T]], 1), cat([rhi, rhi, xlo], 0)))
            pair = group * GROUP + j
            w_buf[pair] = jnp.where(state_lanes, results[0], results[1]) + cat(list(ends[j]), 0)
            add_buf[pair] = pltpu.roll(jnp.where(state_lanes, results[1], results[0]), C, 1)

    def state_copy(pair):
        return pltpu.make_async_remote_copy(
            src_ref=z_out.at[pair],
            dst_ref=z_in.at[pair],
            send_sem=send_sem.at[pair],
            recv_sem=recv_sem.at[pair],
            device_id={"seq": lax.rem(me + 1, members)},
            device_id_type=MESH,
        )

    def relay(group):
        pairs_now = [group * GROUP + j for j in range(GROUP)]

        @pl.when(me == 0)
        def _():
            for pair in pairs_now:
                z_out[pair] = add_buf[pair, T:, :]

        @pl.when(me > 0)
        def _():
            for pair in pairs_now:
                state_copy(pair).wait_recv()
            states = [diagonal_state(z_in[pair]) for pair in pairs_now]
            moved = [product3(w_buf[pair, T:, :], z) for pair, z in zip(pairs_now, states)]
            for pair, product in zip(pairs_now, moved):
                z_out[pair] = product + add_buf[pair, T:, :]

        @pl.when(me < last)
        def _():
            for pair in pairs_now:
                state_copy(pair).start()

        @pl.when(me == last)
        def _():
            for pair in pairs_now:
                s_buf[lanes_of(pair), :] = jnp.transpose(z_out[pair])

    def out_copy(group):
        at = pl.ds(pl.multiple_of(group * (GROUP * LANES), LANES), GROUP * LANES)
        return pltpu.make_async_copy(out_ref.at[:, at], out_hbm.at[:, at], out_sem.at[group])

    def finish(group):
        ones2 = head_ones()
        for j in range(GROUP):
            pair = group * GROUP + j
            at = lanes_of(pair)
            z = diagonal_state(z_in[pair])
            result = product3(w_buf[pair, :T, :], z) + add_buf[pair, :T, :]
            average = head_sum(result, ones2) * (1.0 / C)
            centered = result - average
            spread = head_sum(centered * centered, ones2) * (1.0 / C)
            normed = centered * lax.rsqrt(spread + NORM_EPS) * g_ref[at][None, :]
            bonus = r_ref[:, at].astype(F32) * k_ref[:, at].astype(F32) * u_ref[at][None, :]
            extra = head_sum(bonus, ones2) * v_ref[:, at].astype(F32)
            out_ref[:, at] = (normed + extra).astype(out_ref.dtype)
        out_copy(group).start()

    def final_copy(target):
        return pltpu.make_async_remote_copy(
            src_ref=s_buf.at[pl.ds(pl.multiple_of(target * share, 8), share), :],
            dst_ref=final_ref,
            send_sem=fsend_sem.at[target],
            recv_sem=frecv_sem,
            device_id={"seq": target},
            device_id_type=MESH,
        )

    def own_copy():
        return pltpu.make_async_copy(s_buf.at[pl.ds(last * share, share), :], final_ref, local_sem)

    group_rows = GROUP * LANES
    finish_from = jnp.maximum(me + 1, groups - (me // last) * groups)

    def step(s, _):
        @pl.when(s < groups)
        def _():
            compute(s)

        @pl.when(s == 0)
        def _():
            pl.semaphore_wait(barrier, members - 1)
            for copy in gain_copies:
                copy.wait()

        done = s - finish_from

        @pl.when(jnp.logical_and(done >= 0, done < groups))
        def _():
            finish(done)

        turn = s - me

        @pl.when(jnp.logical_and(turn >= 0, turn < groups))
        def _():
            relay(turn)

            @pl.when(me == last)
            def _():
                for target in range(last):
                    ready = -(-(target + 1) * share // group_rows) - 1

                    @pl.when(turn == ready)
                    def _():
                        final_copy(target).start()

                @pl.when(turn == groups - 1)
                def _():
                    own_copy().start()

        return 0

    lax.fori_loop(0, groups + max(groups, members), step, 0)

    for group in range(groups):
        out_copy(group).wait()

    @pl.when(me == last)
    def _():
        own_copy().wait()
        for target in range(last):
            final_copy(target).wait_send()

    @pl.when(me < last)
    def _():
        final_copy(0).wait_recv()

        def sent(pair, _):
            state_copy(pair).wait_send()
            return 0

        lax.fori_loop(0, pairs, sent, 0)


def hand_on(out_in, final_in, out, final, rows, turned, held, in_sem, out_sem, final_sem):
    T = out.shape[0]
    size = T // PIECES
    arriving = pltpu.make_async_copy(final_in, rows, final_sem.at[0])
    arriving.start()
    parts = [pl.ds(i * size, size) for i in range(PIECES)]
    loads = [
        pltpu.make_async_copy(out_in.at[at, :], held.at[at, :], in_sem.at[i])
        for i, at in enumerate(parts)
    ]
    stores = [
        pltpu.make_async_copy(held.at[at, :], out.at[at, :], out_sem.at[i])
        for i, at in enumerate(parts)
    ]
    for load in loads:
        load.start()
    arriving.wait()
    turned[...] = jnp.transpose(rows[...])
    leaving = pltpu.make_async_copy(turned, final, final_sem.at[1])
    leaving.start()
    for load, store in zip(loads, stores):
        load.wait()
        store.start()
    for store in stores:
        store.wait()
    leaving.wait()


def on_device(r, lf, k, v, e, a, u, g, *, members):
    sequences, T, channels = r.shape
    pairs = channels // LANES
    share = channels // members
    call = pl.pallas_call(
        functools.partial(kernel, members),
        out_shape=(
            jax.ShapeDtypeStruct((T, channels), BF16),
            jax.ShapeDtypeStruct((share, C), F32),
        ),
        in_specs=[pl.BlockSpec(memory_space=pl.ANY)] * 8,
        out_specs=[pl.BlockSpec(memory_space=pl.ANY), pl.BlockSpec(memory_space=pltpu.VMEM)],
        scratch_shapes=[pltpu.VMEM((T, channels), BF16)] * 6
        + [pltpu.VMEM((channels,), F32)] * 2
        + [pltpu.VMEM((T, channels), BF16)]
        + [
            pltpu.VMEM((pairs, T + C, LANES), F32),
            pltpu.VMEM((pairs, T + C, LANES), F32),
            pltpu.VMEM((pairs, C, LANES), F32),
            pltpu.VMEM((pairs, C, LANES), F32),
            pltpu.VMEM((channels, C), F32),
            pltpu.SemaphoreType.DMA((pairs,)),
            pltpu.SemaphoreType.DMA((pairs,)),
            pltpu.SemaphoreType.DMA((members - 1,)),
            pltpu.SemaphoreType.DMA,
            pltpu.SemaphoreType.DMA,
            pltpu.SemaphoreType.DMA((6, pairs // GROUP)),
            pltpu.SemaphoreType.DMA((2,)),
            pltpu.SemaphoreType.DMA((pairs // GROUP,)),
        ],
        compiler_params=pltpu.CompilerParams(
            collective_id=0, has_side_effects=True, vmem_limit_bytes=VMEM_GRANT
        ),
    )
    out, final = call(
        *(x.reshape(T, channels) for x in (r, lf, k, v, e, a)),
        u,
        g,
    )
    out, final = pl.pallas_call(
        hand_on,
        out_shape=(
            jax.ShapeDtypeStruct((T, channels), BF16),
            jax.ShapeDtypeStruct((C, share), F32),
        ),
        in_specs=[pl.BlockSpec(memory_space=pl.ANY)] * 2,
        out_specs=[pl.BlockSpec(memory_space=pl.ANY)] * 2,
        scratch_shapes=[
            pltpu.VMEM((share, C), F32),
            pltpu.VMEM((C, share), F32),
            pltpu.VMEM((T, channels), BF16),
            pltpu.SemaphoreType.DMA((PIECES,)),
            pltpu.SemaphoreType.DMA((PIECES,)),
            pltpu.SemaphoreType.DMA((2,)),
        ],
        compiler_params=pltpu.CompilerParams(vmem_limit_bytes=VMEM_GRANT),
    )(out, final)
    return out.reshape(sequences, T, channels), jnp.transpose(final).reshape(sequences, share, C)


def solution(mesh):
    split_spec = P(("groups", "dp"), "seq", None)
    return jax.shard_map(
        functools.partial(on_device, members=mesh.shape["seq"]),
        mesh=mesh,
        in_specs=(split_spec,) * 6 + (P(), P()),
        out_specs=(split_spec, split_spec),
        check_vma=False,
    )
```
